512 devices in a mesh: space: 16 (over z, core), dp: 32 (over y, x).
Axes of the slice: x: 4, y: 8, z: 8, core: 2. Of those that a mesh axis runs over, the one named last changes fastest.
Arguments:
- volumes: bfloat16 [32, 64, 32, 16, 128], P('dp', None, 'space'), may hold values from -6 to 6
- w_first: bfloat16 [3, 3, 3, 64, 64], replicated, may hold values from -0.15625 to 0.15625
- w_down: bfloat16 [2, 2, 2, 64, 64], replicated, may hold values from -0.25 to 0.25
- w_coarse: bfloat16 [3, 3, 3, 64, 64], replicated, may hold values from -0.15625 to 0.15625
- coarse_cotangent: bfloat16 [32, 64, 16, 8, 64], P('dp', None, 'space'), may hold values from -6 to 6
Outputs:
- coarse_out: bfloat16 [32, 64, 16, 8, 64], P('dp', None, 'space')
- grad_first: float32 [3, 3, 3, 64, 64], replicated
- grad_down: float32 [2, 2, 2, 64, 64], replicated
- grad_coarse: float32 [3, 3, 3, 64, 64], replicated
The draws below stay inside these ranges and needn't reach their ends.
All inputs are finite; a program needn't handle non-finite values.
Results may differ from the reference program's by a relative error of at most 0.015.
Values may be sent and summed in bfloat16 or wider, within the bound.
No kernel may reach another device: no remote copies, remote signals or barrier semaphores. Data moves between devices by JAX's collectives and lax.ppermute only.
A program may use at most 64 MiB of HBM per device.

```python
import jax
import jax.numpy as jnp
from jax import lax

C = 64
Y = 16
Z = 128
B = 32
NX = 32


def shard_levels(stream_key, shape, pieces, smallest, largest):
    factor_of = 1.0
    for dim, parts in pieces:
        heights = jax.random.uniform(jax.random.fold_in(jax.random.fold_in(stream_key, 6), dim), (parts,), jnp.float32, smallest / len(pieces), largest / len(pieces))
        factor_of = factor_of * jnp.repeat(jnp.exp(heights), shape[dim] // parts).reshape((-1,) + (1,) * (len(shape) - 1 - dim))
    return factor_of


def normal_values(own_key, shape, scale, limit, shards=(), dtype=jnp.bfloat16):
    array = scale * jax.random.normal(own_key, shape, jnp.float32)
    if shards:
        array = array * shard_levels(own_key, shape, shards, -0.22, 0.18)
    return jnp.clip(array, -limit, limit).astype(dtype)


def setup_inputs(seed: int = 0) -> dict:
    arg_keys = jax.random.split(jax.random.key(seed), 6)
    return {
        "volumes": normal_values(arg_keys[0], (B, C, NX, Y, Z), 1.0, 6.0, ((0, 32), (2, 16))),
        "w_first": normal_values(arg_keys[1], (3, 3, 3, C, C), (27 * C) ** -0.5, 0.15625),
        "w_down": normal_values(arg_keys[2], (2, 2, 2, C, C), (8 * C) ** -0.5, 0.25),
        "w_coarse": normal_values(arg_keys[3], (3, 3, 3, C, C), (27 * C) ** -0.5, 0.15625),
        "coarse_cotangent": normal_values(arg_keys[4], (B, C, NX // 2, Y // 2, Z // 2), 1.0, 6.0, ((0, 32), (2, 16))),
    }


conv_layout = ('NCDHW', 'DHWIO', 'NCDHW')

def pad_all(field):
    return jnp.pad(field, ((0, 0), (0, 0), (1, 1), (1, 1), (1, 1)))

def conv_cube(padded, weight):
    return lax.conv_general_dilated(padded.astype(jnp.float32), weight.astype(jnp.float32), (1, 1, 1), 'VALID', dimension_numbers=conv_layout, preferred_element_type=jnp.float32)

def conv_down(field, weight):
    return lax.conv_general_dilated(field.astype(jnp.float32), weight.astype(jnp.float32), (2, 2, 2), 'VALID', dimension_numbers=conv_layout, preferred_element_type=jnp.float32)

def kernel_grad(padded, grads, dilation):
    return lax.conv_general_dilated(padded.astype(jnp.float32), grads.astype(jnp.float32), (1, 1, 1), 'VALID', rhs_dilation=dilation, dimension_numbers=('CNDHW', 'IODHW', 'DHWNC'), preferred_element_type=jnp.float32)

def silu_slope(value):
    sigmoid_val = jax.nn.sigmoid(value)
    return sigmoid_val * (1.0 + value * (1.0 - sigmoid_val))

def flipped(weight):
    return jnp.swapaxes(weight[::-1, ::-1, ::-1], 3, 4)

def up_sample(grads, weight):
    spread = jnp.einsum('bopqr,xyzio->bipxqyrz', grads.astype(jnp.float32), weight.astype(jnp.float32))
    shape = grads.shape
    return spread.reshape(shape[0], weight.shape[3], 2 * shape[2], 2 * shape[3], 2 * shape[4])

def reference(volumes, w_first, w_down, w_coarse, coarse_cotangent):

    def one_volume(carry, items):
        volume, cotangent = items
        volume = volume[None]
        cotangent = cotangent[None]
        padded_in = pad_all(volume)
        first_pre = conv_cube(padded_in, w_first)
        first_act = jax.nn.silu(first_pre).astype(jnp.bfloat16)
        down_out = conv_down(first_act, w_down).astype(jnp.bfloat16)
        padded_down = pad_all(down_out)
        coarse_pre = conv_cube(padded_down, w_coarse)
        coarse_out = jax.nn.silu(coarse_pre).astype(jnp.bfloat16)
        coarse_grad = (cotangent.astype(jnp.float32) * silu_slope(coarse_pre)).astype(jnp.bfloat16)
        grad_coarse = kernel_grad(padded_down, coarse_grad, (1, 1, 1))
        down_grad = conv_cube(pad_all(coarse_grad), flipped(w_coarse)).astype(jnp.bfloat16)
        grad_down = kernel_grad(first_act, down_grad, (2, 2, 2))
        first_grad = (up_sample(down_grad, w_down) * silu_slope(first_pre)).astype(jnp.bfloat16)
        grad_first = kernel_grad(padded_in, first_grad, (1, 1, 1))
        totals = (carry[0] + grad_first, carry[1] + grad_down, carry[2] + grad_coarse)
        return (totals, coarse_out[0])
    start = (jnp.zeros(w_first.shape, jnp.float32), jnp.zeros(w_down.shape, jnp.float32), jnp.zeros(w_coarse.shape, jnp.float32))
    totals, coarse_out = lax.scan(one_volume, start, (volumes, coarse_cotangent))
    return (coarse_out, totals[0], totals[1], totals[2])
```

```python
import jax
import jax.numpy as jnp
from jax import lax
from jax.experimental import pallas as pl
from jax.experimental.pallas import tpu as pltpu
from jax.sharding import PartitionSpec as P

F32, BF16 = jnp.float32, jnp.bfloat16
PARAMS = pltpu.CompilerParams(vmem_limit_bytes=48 * 1024 * 1024)
NN = (((1,), (0,)), ((), ()))
NT = (((1,), (1,)), ((), ()))


def dot(a, b, dims=NN):
    return lax.dot_general(a, b, dims, preferred_element_type=F32)


def low_lanes(shape):
    return lax.broadcasted_iota(jnp.int32, shape, 1) < 64


def pick_matrix():
    row = lax.broadcasted_iota(jnp.int32, (256, 128), 0)
    col = lax.broadcasted_iota(jnp.int32, (256, 128), 1)
    return (2 * (row % 64) - 1 + row // 64 == col).astype(F32).astype(BF16)


def twice():
    row = lax.broadcasted_iota(jnp.int32, (64, 128), 0)
    col = lax.broadcasted_iota(jnp.int32, (64, 128), 1)
    return (row == col % 64).astype(F32).astype(BF16)


def gather_taps(plane, out):
    picked = dot(pick_matrix(), plane, NT).astype(BF16)
    for y in range(8):
        for tz in range(4):
            out[y * 64 : y * 64 + 64, tz * 128 : tz * 128 + 128] = picked[
                tz * 64 : tz * 64 + 64, y * 128 : y * 128 + 128
            ]
    low = low_lanes((64, 128))
    zero = jnp.zeros((64, 128), BF16)
    for y in range(8):
        for tz in range(4):
            block = picked[tz * 64 : tz * 64 + 64]
            above = block[:, y * 128 - 128 : y * 128] if y > 0 else zero
            below = block[:, y * 128 + 128 : y * 128 + 256] if y < 7 else zero
            out[y * 64 : y * 64 + 64, 512 + tz * 128 : 640 + tz * 128] = jnp.where(
                low, below, above
            )


def gather_coarse(field, out):
    row = lax.broadcasted_iota(jnp.int32, (512, 128), 0) % 64
    low = low_lanes((512, 128))
    before = jnp.where(row == 0, 0.0, pltpu.roll(field, 1, 0))
    after = jnp.where(row == 63, 0.0, pltpu.roll(field, 511, 0))
    sides = jnp.where(low, before, after).astype(BF16)
    mid = field.astype(BF16)
    zero = jnp.zeros((64, 128), BF16)
    up = jnp.concatenate([zero, field[:448].astype(BF16)], 0)
    down = jnp.concatenate([field[64:].astype(BF16), zero], 0)
    out[0:64, 0:128] = zero
    out[64:512, 0:128] = sides[:448]
    out[:, 128:256] = sides
    out[0:448, 256:384] = sides[64:]
    out[448:512, 256:384] = zero
    out[:, 384:512] = jnp.where(low, up, down)
    out[:, 512:640] = mid


def prepare_kernel(own, w_first, w_down, w_coarse, cot, part, fw, dw, cw, bw, taps):
    low = low_lanes((64, 128))
    zero = jnp.zeros((64, 128), BF16)
    pair = twice()

    def both(ref, k):
        return dot(ref[k * 64 : k * 64 + 64], pair).astype(BF16)

    for dx in range(3):
        for tz in range(4):
            for qz in range(2):
                iz = tz - qz
                w = [both(w_first, dx * 9 + iy * 3 + iz) for iy in range(3)] if 0 <= iz < 3 else None
                for side in range(2):
                    at = side * 512 + tz * 128
                    lanes = slice(qz * 128, qz * 128 + 128)
                    if w is None:
                        first = second = zero
                    elif side == 0:
                        first = jnp.where(low, w[1], w[0])
                        second = jnp.where(low, w[2], w[1])
                    else:
                        first = jnp.where(low, zero, w[2])
                        second = jnp.where(low, w[0], zero)
                    fw[dx, at : at + 64, lanes] = first
                    fw[dx, at + 64 : at + 128, lanes] = second
    for x in range(2):
        for qz in range(2):
            for qy in range(2):
                k = x * 4 + qy * 2 + qz
                at = (x * 4 + qz * 2 + qy) * 64
                dw[at : at + 64] = both(w_down, k)
    order = [(0, 0), (0, 2), (1, 0), (1, 2), (2, 0), (2, 2), (0, 1), (2, 1), (1, 1), None]
    for dx in range(3):
        back = []
        for j, tap in enumerate(order):
            at = dx * 640 + j * 64
            if tap is None:
                cw[at : at + 64] = zero
                back.append(zero)
            else:
                cw[at : at + 64] = both(w_coarse, dx * 9 + tap[0] * 3 + tap[1])
                back.append(both(w_coarse, (2 - dx) * 9 + (2 - tap[0]) * 3 + 2 - tap[1]))
        for j in range(5):
            at = dx * 640 + j * 128
            bw[:, at : at + 128] = jnp.where(low, back[2 * j], back[2 * j + 1])
    for x in range(2):
        gather_taps(own[x * 1024 : x * 1024 + 1024], taps.at[x])
    part[0] = dot(taps[0], fw[1]) + dot(taps[1], fw[2])
    part[1] = dot(taps[0], fw[0]) + dot(taps[1], fw[1])


def first_kernel(before, after, part, fw, dw, act, slope, send, taps):
    low = low_lanes((256, 128))
    for x, side in enumerate((before, after)):
        gather_taps(side[0:1024], taps)
        pre = part[x] + dot(taps[...], fw[2 * x])
        s = jax.nn.sigmoid(pre)
        act[:, x * 256 : x * 256 + 256] = (pre * s).astype(BF16)
        slope[:, x * 256 : x * 256 + 256] = s * (1.0 + pre * (1.0 - s))
    down = dot(act[...], dw[...])
    send[...] = jnp.where(low, down[:256], down[256:]).astype(BF16)


def rest_kernel(
    d0, d1, d2, d3, d4, own, before, after, cot, act, slope, dw, cw, bw, out, grads, taps, near, near2
):
    low = low_lanes((64, 128))
    low2 = low_lanes((256, 128))
    pair = twice()
    for p, ref in enumerate((d0, d1, d2, d3, d4)):
        field = ref[...].astype(F32)
        turned = pltpu.roll(field, 64, 1)
        field = jnp.concatenate(
            [jnp.where(low2, field, turned), jnp.where(low2, turned, field)], 0
        )
        gather_coarse(field, near.at[p])
    mid = None
    for p in range(3):
        pre = dot(near[p], cw[0:640]) + dot(near[p + 1], cw[640:1280]) + dot(near[p + 2], cw[1280:1920])
        s = jax.nn.sigmoid(pre)
        if p == 1:
            silu = (pre * s).T
            out[...] = silu[0:64].astype(BF16)
        source = (before, cot, after)[p]
        base = 0 if p == 1 else 1024
        ct = jnp.concatenate(
            [
                source[base + j * 64 : base + j * 64 + 64].astype(F32).T.astype(BF16)
                for j in range(4)
            ],
            0,
        )
        grad = (dot(ct, pair) * (s * (1.0 + pre * (1.0 - s)))).astype(BF16).astype(F32)
        if p == 1:
            mid = grad
        gather_coarse(grad, near2.at[p])
    mid_t = mid.T[0:64].astype(BF16)
    center = []
    for dx in range(3):
        g = dot(mid_t, near[dx + 1])
        for j in range(4):
            at = (14 + dx * 4 + j) * 64
            grads[at : at + 64] = g[:, j * 128 : j * 128 + 128].astype(BF16)
        center.append(g[:, 512:640])
    grads[26 * 64 : 27 * 64] = jnp.where(low, center[0], center[1]).astype(BF16)
    grads[27 * 64 : 28 * 64] = center[2].astype(BF16)
    down_grad = (
        dot(near2[0], bw[:, 0:640], NT)
        + dot(near2[1], bw[:, 640:1280], NT)
        + dot(near2[2], bw[:, 1280:1920], NT)
    )
    dg = down_grad.astype(BF16)
    dg_t = down_grad.T.astype(BF16)
    gd = dot(dg_t, act[...])
    for j in range(4):
        at = (28 + j) * 64
        grads[at : at + 64] = gd[:, j * 128 : j * 128 + 128].astype(BF16)
    fg = dot(dg, dw[:, 0:64], NT) * slope[...]
    fg_t = fg.T.astype(BF16)
    for p, plane in enumerate((before[0:1024], own[0:1024], own[1024:2048], after[0:1024])):
        gather_taps(plane, taps.at[p])
    mids, zero_y = [], []
    for dx in range(3):
        g = dot(fg_t[0:256], taps[dx]) + dot(fg_t[256:512], taps[dx + 1])
        for iz in range(3):

            def summed(side, qy):
                at = side * 512 + iz * 128
                return (
                    g[qy * 64 : qy * 64 + 64, at : at + 128]
                    + g[128 + qy * 64 : 192 + qy * 64, at + 128 : at + 256]
                )

            z0, z1, u0, u1 = summed(0, 0), summed(0, 1), summed(1, 0), summed(1, 1)
            j = dx * 3 + iz
            grads[j * 64 : j * 64 + 64] = (
                z0 + pltpu.roll(jnp.where(low, u1, z1), 64, 1)
            ).astype(BF16)
            zero_y.append((z1, u0))
    zero_y.append((jnp.zeros((64, 128), F32),) * 2)
    for m in range(5):
        (z1a, u0a), (z1b, u0b) = zero_y[2 * m], zero_y[2 * m + 1]
        at = (9 + m) * 64
        grads[at : at + 64] = (
            jnp.where(low, z1a, u0b) + pltpu.roll(jnp.where(low, z1b, u0a), 64, 1)
        ).astype(BF16)


def unpack_kernel(packed, first, down, coarse):
    def block(b):
        return packed[b * 64 : b * 64 + 64].astype(F32).T

    for j in range(9):
        dx, iz = j // 3, j % 3
        t = block(j)
        first[dx, 1, iz] = t[0:64]
        first[dx, 2, iz] = t[64:128]
    for m in range(5):
        t = block(9 + m)
        for h in range(2):
            j = 2 * m + h
            if j < 9:
                first[j // 3, 0, j % 3] = t[h * 64 : h * 64 + 64]
    pairs = [((0, 0), (0, 2)), ((1, 0), (1, 2)), ((2, 0), (2, 2)), ((0, 1), (2, 1))]
    for dx in range(3):
        for j in range(4):
            t = block(14 + dx * 4 + j)
            for h in range(2):
                dy, dz = pairs[j][h]
                coarse[dx, dy, dz] = t[h * 64 : h * 64 + 64]
    t = block(26)
    coarse[0, 1, 1] = t[0:64]
    coarse[1, 1, 1] = t[64:128]
    coarse[2, 1, 1] = block(27)[0:64]
    for j in range(4):
        t = block(28 + j)
        for qy in range(2):
            down[j // 2, qy, j % 2] = t[qy * 64 : qy * 64 + 64]


def call(kernel, outs, scratch=()):
    return pl.pallas_call(
        kernel,
        out_shape=[jax.ShapeDtypeStruct(s, d) for s, d in outs],
        scratch_shapes=[pltpu.VMEM(s, d) for s, d in scratch],
        compiler_params=PARAMS,
    )


def swap(y, axis):
    return lax.all_to_all(y, axis, 0, 0, tiled=True)


def total(part):
    space, dp = lax.axis_size("space"), lax.axis_size("dp")
    rows = part.shape[0]
    y = swap(part.reshape(dp, rows // dp, 128), "dp")
    y = jnp.sum(y.astype(F32), 0).astype(BF16)
    y = swap(y.reshape(space, rows // dp // space, 128), "space")
    y = jnp.sum(y.astype(F32), 0).astype(BF16)
    y = swap(jnp.broadcast_to(y[None], (space,) + y.shape), "space").reshape(rows // dp, 128)
    return swap(jnp.broadcast_to(y[None], (dp,) + y.shape), "dp").reshape(rows, 128)


def local(volumes, w_first, w_down, w_coarse, cotangent):
    n = lax.axis_size("space")

    def shift(value, by):
        steps = [(i, i + by) for i in range(n) if 0 <= i + by < n]
        return lax.ppermute(value, "space", steps)

    own = jnp.transpose(volumes[0], (1, 2, 0, 3)).reshape(2048, 128)
    cot = jnp.transpose(cotangent.reshape(64, 4, 128), (1, 0, 2)).reshape(256, 128)
    before = shift(jnp.concatenate([own[1024:], cot]), 1)
    after = shift(jnp.concatenate([own[:1024], cot]), -1)
    part, fw, dw, cw, bw = call(
        prepare_kernel,
        [((2, 512, 256), F32), ((3, 1024, 256), BF16), ((512, 128), BF16), ((1920, 128), BF16), ((64, 1920), BF16)],
        [((2, 512, 1024), BF16)],
    )(own, w_first.reshape(1728, 64), w_down.reshape(512, 64), w_coarse.reshape(1728, 64), cot)
    act, slope, down = call(
        first_kernel,
        [((512, 512), BF16), ((512, 512), F32), ((256, 128), BF16)],
        [((512, 1024), BF16)],
    )(before, after, part, fw, dw)
    halo = [shift(down, 2), shift(down, 1), down, shift(down, -1), shift(down, -2)]
    out, grads = call(
        rest_kernel,
        [((64, 512), BF16), ((2048, 128), BF16)],
        [((4, 512, 1024), BF16), ((5, 512, 640), BF16), ((3, 512, 640), BF16)],
    )(*halo, own, before, after, cot, act, slope, dw, cw, bw)
    first, down_w, coarse = call(
        unpack_kernel,
        [((3, 3, 3, 64, 64), F32), ((2, 2, 2, 64, 64), F32), ((3, 3, 3, 64, 64), F32)],
    )(total(grads))
    return (out.reshape(1, 64, 1, 8, 64), first, down_w, coarse)


def solution(mesh):
    return jax.shard_map(
        local,
        mesh=mesh,
        in_specs=(
            P("dp", None, "space", None, None),
            P(),
            P(),
            P(),
            P("dp", None, "space", None, None),
        ),
        out_specs=(P("dp", None, "space", None, None), P(), P(), P()),
        check_vma=False,
    )
```

```python
import jax
import jax.numpy as jnp
from jax import lax
from jax.experimental import pallas as pl
from jax.experimental.pallas import tpu as pltpu
from jax.sharding import PartitionSpec as P

F32, BF16 = jnp.float32, jnp.bfloat16
PARAMS = pltpu.CompilerParams(vmem_limit_bytes=32 * 1024 * 1024)
NN = (((1,), (0,)), ((), ()))
NT = (((1,), (1,)), ((), ()))


def dot(a, b, dims=NN):
    return lax.dot_general(a, b, dims, preferred_element_type=F32)


def low_lanes(shape):
    return lax.broadcasted_iota(jnp.int32, shape, 1) < 64


def pick_matrix():
    row = lax.broadcasted_iota(jnp.int32, (256, 128), 0)
    col = lax.broadcasted_iota(jnp.int32, (256, 128), 1)
    return (2 * (row % 64) - 1 + row // 64 == col).astype(F32).astype(BF16)


def twice():
    row = lax.broadcasted_iota(jnp.int32, (64, 128), 0)
    col = lax.broadcasted_iota(jnp.int32, (64, 128), 1)
    return (row == col % 64).astype(F32).astype(BF16)


def gather_taps(plane, out):
    picked = dot(pick_matrix(), plane, NT).astype(BF16)
    low = low_lanes((64, 128))
    zero = jnp.zeros((64, 128), BF16)
    for y in range(8):
        for tz in range(4):
            block = picked[tz * 64 : tz * 64 + 64]
            above = block[:, y * 128 - 128 : y * 128] if y > 0 else zero
            below = block[:, y * 128 + 128 : y * 128 + 256] if y < 7 else zero
            rows = slice(y * 64, y * 64 + 64)
            out[rows, tz * 128 : tz * 128 + 128] = block[:, y * 128 : y * 128 + 128]
            out[rows, 512 + tz * 128 : 640 + tz * 128] = jnp.where(low, below, above)


def gather_coarse(field, out):
    row = lax.broadcasted_iota(jnp.int32, (512, 128), 0) % 64
    low = low_lanes((512, 128))
    before = jnp.where(row == 0, 0.0, pltpu.roll(field, 1, 0))
    after = jnp.where(row == 63, 0.0, pltpu.roll(field, 511, 0))
    sides = jnp.where(low, before, after).astype(BF16)
    mid = field.astype(BF16)
    zero = jnp.zeros((64, 128), BF16)
    up = jnp.concatenate([zero, mid[:448]], 0)
    down = jnp.concatenate([mid[64:], zero], 0)
    out[0:64, 0:128] = zero
    out[64:512, 0:128] = sides[:448]
    out[:, 128:256] = sides
    out[0:448, 256:384] = sides[64:]
    out[448:512, 256:384] = zero
    out[:, 384:512] = jnp.where(low, up, down)
    out[:, 512:640] = mid


def turned(ref):
    field = ref.astype(F32)
    return field, pltpu.roll(field, 64, 1)


def doubled(ref):
    field, swapped = turned(ref)
    low = low_lanes((256, 128))
    return jnp.concatenate([jnp.where(low, field, swapped), jnp.where(low, swapped, field)], 0)


def edges_kernel(volumes, cot, first, last, planes, rows):
    for x, out in enumerate((first, last)):
        planes[x] = volumes[:, x].astype(F32).reshape(1024, 128)
        for y in range(16):
            out[y * 64 : y * 64 + 64] = planes[x, pl.ds(y, 64, stride=16), :].astype(BF16)
    rows[...] = cot[...].astype(F32).reshape(512, 64)
    for j in range(4):
        both = jnp.concatenate(
            [rows[pl.ds(j, 64, stride=8), :], rows[pl.ds(j + 4, 64, stride=8), :]], 0
        )
        block = both.T.astype(BF16)
        for out in (first, last):
            out[1024 + j * 64 : 1088 + j * 64] = block


def prepare_kernel(first, last, w_first, w_down, w_coarse, part, fw, dw, cw, bw, taps):
    low = low_lanes((64, 128))
    zero = jnp.zeros((64, 128), BF16)
    pair = twice()

    def both(ref, k):
        return dot(ref[k * 64 : k * 64 + 64], pair).astype(BF16)

    for dx in range(3):
        for tz in range(4):
            for qz in range(2):
                iz = tz - qz
                w = [both(w_first, dx * 9 + iy * 3 + iz) for iy in range(3)] if 0 <= iz < 3 else None
                for side in range(2):
                    at = dx * 1024 + side * 512 + tz * 128
                    lanes = slice(qz * 128, qz * 128 + 128)
                    if w is None:
                        upper = lower = zero
                    elif side == 0:
                        upper = jnp.where(low, w[1], w[0])
                        lower = jnp.where(low, w[2], w[1])
                    else:
                        upper = jnp.where(low, zero, w[2])
                        lower = jnp.where(low, w[0], zero)
                    fw[at : at + 64, lanes] = upper
                    fw[at + 64 : at + 128, lanes] = lower
    for x in range(2):
        for qz in range(2):
            for qy in range(2):
                k = x * 4 + qy * 2 + qz
                at = (x * 4 + qz * 2 + qy) * 64
                dw[at : at + 64] = both(w_down, k)
    order = [(0, 0), (0, 2), (1, 0), (1, 2), (2, 0), (2, 2), (0, 1), (2, 1), (1, 1), None]
    for j, tap in enumerate(order):
        if tap is None:
            w = [zero] * 3
        else:
            w = [both(w_coarse, dx * 9 + tap[0] * 3 + tap[1]) for dx in range(3)]
        w = [zero] * 2 + w + [zero] * 2
        for p in range(5):
            at = p * 640 + j * 64
            cw[at : at + 64, 0:128] = jnp.where(low, w[p + 2], w[p + 1])
            cw[at : at + 64, 128:256] = jnp.where(low, w[p], zero)
    for dx in range(3):
        back = [
            zero if tap is None else both(w_coarse, (2 - dx) * 9 + (2 - tap[0]) * 3 + 2 - tap[1])
            for tap in order
        ]
        for j in range(5):
            at = dx * 640 + j * 128
            bw[:, at : at + 128] = jnp.where(low, back[2 * j], back[2 * j + 1])
    for x, ref in enumerate((first, last)):
        gather_taps(ref[0:1024], taps.at[:, x * 1024 : x * 1024 + 1024])
    for x in range(2):
        part[x * 512 : x * 512 + 512] = dot(taps[...], fw[1024 - x * 1024 : 3072 - x * 1024])


def first_kernel(before, after, part, fw, dw, act, pre, send, taps):
    low = low_lanes((256, 128))
    for x, side in enumerate((before, after)):
        gather_taps(side[0:1024], taps)
        value = part[x * 512 : x * 512 + 512] + dot(taps[...], fw[x * 2048 : x * 2048 + 1024])
        pre[x * 512 : x * 512 + 512] = value
        act[:, x * 256 : x * 256 + 256] = (value * jax.nn.sigmoid(value)).astype(BF16)
    down = dot(act[...], dw[...])
    send[...] = jnp.where(low, down[:256], down[256:]).astype(BF16)


def beside_kernel(first, last, before, after, pre, down, cw, taps, slope, ct, own, acc):
    value = pre[...]
    s = jax.nn.sigmoid(value)
    slope[...] = s * (1.0 + value * (1.0 - s))
    for p, ref in enumerate((before, first, last, after)):
        gather_taps(ref[0:1024], taps.at[p * 512 : p * 512 + 512])
    low = low_lanes((256, 128))
    f0, t0 = turned(before[1024:1280])
    f1, t1 = turned(first[1024:1280])
    f2, t2 = turned(after[1024:1280])
    ct[0:256, 0:128] = jnp.where(low, f0, t1)
    ct[256:512, 0:128] = jnp.where(low, t0, f1)
    ct[0:256, 128:256] = f2
    ct[256:512, 128:256] = t2
    gather_coarse(doubled(down[...]), own)
    acc[...] = dot(own[...], cw[1280:1920])


def rest_kernel(
    core, d0, d1, d3, d4, act, slope, taps, ct, own, acc, dw, cw, bw, out, keep, send, grads, below, above, near
):
    low = low_lanes((64, 128))
    for p, ref in enumerate((d0, d1)):
        gather_coarse(doubled(ref[...]), below.at[:, p * 640 : p * 640 + 640])
    for p, ref in enumerate((d3, d4)):
        gather_coarse(doubled(ref[...]), above.at[:, p * 640 : p * 640 + 640])
    pre = acc[...] + dot(below[...], cw[0:1280]) + dot(above[...], cw[1920:3200])
    s = jax.nn.sigmoid(pre)
    out[...] = (pre[:, 0:128] * s[:, 0:128]).T[64:128].astype(BF16)
    grad = (ct[...] * (s * (1.0 + pre * (1.0 - s)))).astype(BF16).astype(F32)
    two, one = grad[:, 0:128], grad[:, 128:256]
    two_t, one_t = pltpu.roll(two, 64, 1), pltpu.roll(one, 64, 1)
    low2 = low_lanes((512, 128))
    gather_coarse(jnp.where(low2, two, two_t), near.at[:, 0:640])
    gather_coarse(jnp.where(low2, two_t, two), near.at[:, 640:1280])
    gather_coarse(jnp.where(low2, one, one_t), near.at[:, 1280:1920])
    dg_wide = dot(near[...], bw[...], NT)
    dg = dg_wide.astype(BF16)
    up = dot(dg, dw[:, 0:64], NT)
    fg_t = jnp.concatenate(
        [
            (up[:, x * 256 : x * 256 + 256] * slope[x * 512 : x * 512 + 512]).T.astype(BF16)
            for x in range(2)
        ],
        1,
    )
    mid_t = two.T[64:128].astype(BF16)
    center = []
    for dx, planes in enumerate((below[:, 640:1280], own[...], above[:, 0:640])):
        g = dot(mid_t, planes)
        for j in range(4):
            at = (14 + dx * 4 + j) * 64
            grads[at : at + 64] = g[:, j * 128 : j * 128 + 128].astype(BF16)
        center.append(g[:, 512:640])
    grads[26 * 64 : 27 * 64] = jnp.where(low, center[0], center[1]).astype(BF16)
    grads[27 * 64 : 28 * 64] = center[2].astype(BF16)
    gd = dot(dg_wide.T.astype(BF16), act[...])
    for j in range(4):
        at = (28 + j) * 64
        grads[at : at + 64] = gd[:, j * 128 : j * 128 + 128].astype(BF16)
    zero_y = []
    for dx in range(3):
        g = dot(fg_t, taps[dx * 512 : dx * 512 + 1024])
        for iz in range(3):

            def summed(side, qy):
                at = side * 512 + iz * 128
                return (
                    g[qy * 64 : qy * 64 + 64, at : at + 128]
                    + g[128 + qy * 64 : 192 + qy * 64, at + 128 : at + 256]
                )

            z0, z1, u0, u1 = summed(0, 0), summed(0, 1), summed(1, 0), summed(1, 1)
            j = dx * 3 + iz
            grads[j * 64 : j * 64 + 64] = (
                z0 + pltpu.roll(jnp.where(low, u1, z1), 64, 1)
            ).astype(BF16)
            zero_y.append((z1, u0))
    zero_y.append((jnp.zeros((64, 128), F32),) * 2)
    for m in range(5):
        (z1a, u0a), (z1b, u0b) = zero_y[2 * m], zero_y[2 * m + 1]
        at = (9 + m) * 64
        grads[at : at + 64] = (
            jnp.where(low, z1a, u0b) + pltpu.roll(jnp.where(low, z1b, u0a), 64, 1)
        ).astype(BF16)
    here = pl.multiple_of(core[0] * 1024, 1024)
    keep[...] = grads[pl.ds(here, 1024), :]
    send[...] = grads[pl.ds(pl.multiple_of(1024 - here, 1024), 1024), :]


def unpack_kernel(core, mine, other, first, down, coarse, packed):
    here = pl.multiple_of(core[0] * 1024, 1024)
    packed[pl.ds(here, 1024), :] = mine[...]
    packed[pl.ds(pl.multiple_of(1024 - here, 1024), 1024), :] = other[...]

    def block(b):
        return packed[b * 64 : b * 64 + 64].astype(F32).T

    for j in range(9):
        dx, iz = j // 3, j % 3
        t = block(j)
        first[dx, 1, iz] = t[0:64]
        first[dx, 2, iz] = t[64:128]
    for m in range(5):
        t = block(9 + m)
        for h in range(2):
            j = 2 * m + h
            if j < 9:
                first[j // 3, 0, j % 3] = t[h * 64 : h * 64 + 64]
    pairs = [((0, 0), (0, 2)), ((1, 0), (1, 2)), ((2, 0), (2, 2)), ((0, 1), (2, 1))]
    for dx in range(3):
        for j in range(4):
            t = block(14 + dx * 4 + j)
            for h in range(2):
                dy, dz = pairs[j][h]
                coarse[dx, dy, dz] = t[h * 64 : h * 64 + 64]
    t = block(26)
    coarse[0, 1, 1] = t[0:64]
    coarse[1, 1, 1] = t[64:128]
    coarse[2, 1, 1] = block(27)[0:64]
    for j in range(4):
        t = block(28 + j)
        for qy in range(2):
            down[j // 2, qy, j % 2] = t[qy * 64 : qy * 64 + 64]


def call(kernel, outs, scratch=(), scalars=0):
    specs = {}
    if scalars:
        specs["in_specs"] = [pl.BlockSpec(memory_space=pltpu.SMEM)] + [
            pl.BlockSpec(memory_space=pltpu.VMEM)
        ] * (scalars - 1)
    return pl.pallas_call(
        kernel,
        out_shape=[jax.ShapeDtypeStruct(s, d) for s, d in outs],
        scratch_shapes=[pltpu.VMEM(s, d) for s, d in scratch],
        compiler_params=PARAMS,
        **specs,
    )


def scatter_sum(y, axis, count, groups=None):
    y = y.reshape(count, y.shape[0] // count, 128)
    y = lax.all_to_all(y, axis, 0, 0, tiled=True, axis_index_groups=groups)
    return jnp.sum(y.astype(F32), 0).astype(BF16)


def spread(y, axis, count, groups=None):
    y = jnp.broadcast_to(y[None], (count,) + y.shape)
    return lax.all_to_all(y, axis, 0, 0, tiled=True, axis_index_groups=groups)


def local(volumes, w_first, w_down, w_coarse, cotangent):
    n, m = lax.axis_size("space"), lax.axis_size("dp")

    def shift(value, by):
        steps = [(i, i + by) for i in range(n) if 0 <= i + by < n]
        return lax.ppermute(value, "space", steps)

    def partner(value):
        return lax.ppermute(value, "space", [(i, i ^ 1) for i in range(n)])

    first, last = call(
        edges_kernel,
        [((1280, 128), BF16)] * 2,
        [((2, 1024, 128), F32), ((512, 64), F32)],
    )(volumes.reshape(64, 2, 16, 128), cotangent.reshape(64, 8, 64))
    before = shift(last, 1)
    after = shift(first, -1)
    part, fw, dw, cw, bw = call(
        prepare_kernel,
        [((1024, 256), F32), ((3072, 256), BF16), ((512, 128), BF16), ((3200, 256), BF16), ((64, 1920), BF16)],
        [((512, 2048), BF16)],
    )(first, last, w_first.reshape(1728, 64), w_down.reshape(512, 64), w_coarse.reshape(1728, 64))
    act, pre, down = call(
        first_kernel,
        [((512, 512), BF16), ((1024, 256), F32), ((256, 128), BF16)],
        [((512, 1024), BF16)],
    )(before, after, part, fw, dw)
    halo = [shift(down, 2), shift(down, 1), shift(down, -1), shift(down, -2)]
    taps, slope, ct, own, acc = call(
        beside_kernel,
        [((2048, 1024), BF16), ((1024, 256), F32), ((512, 256), F32), ((512, 640), BF16), ((512, 256), F32)],
    )(first, last, before, after, pre, down, cw)
    core = lax.rem(lax.axis_index("space"), 2).reshape(1)
    out, keep, send = call(
        rest_kernel,
        [((64, 512), BF16), ((1024, 128), BF16), ((1024, 128), BF16)],
        [((2048, 128), BF16), ((512, 1280), BF16), ((512, 1280), BF16), ((512, 1920), BF16)],
        scalars=14,
    )(core, *halo, act, slope, taps, ct, own, acc, dw, cw, bw)
    half = (keep.astype(F32) + partner(send).astype(F32)).astype(BF16)
    chips = [list(range(c, n, 2)) for c in range(2)]
    piece = scatter_sum(half, "dp", m)
    piece = jnp.sum(spread(piece, "space", n // 2, chips).astype(F32), 0).astype(BF16)
    mine = spread(piece, "dp", m).reshape(1024, 128)
    grad_first, grad_down, grad_coarse = call(
        unpack_kernel,
        [((3, 3, 3, 64, 64), F32), ((2, 2, 2, 64, 64), F32), ((3, 3, 3, 64, 64), F32)],
        [((2048, 128), BF16)],
        scalars=3,
    )(core, mine, partner(mine))
    return (out.reshape(1, 64, 1, 8, 64), grad_first, grad_down, grad_coarse)


def solution(mesh):
    return jax.shard_map(
        local,
        mesh=mesh,
        in_specs=(
            P("dp", None, "space", None, None),
            P(),
            P(),
            P(),
            P("dp", None, "space", None, None),
        ),
        out_specs=(P("dp", None, "space", None, None), P(), P(), P()),
        check_vma=False,
    )
```

```python
import jax
import jax.numpy as jnp
from jax import lax
from jax.experimental import pallas as pl
from jax.experimental.pallas import tpu as pltpu
from jax.sharding import PartitionSpec as P

F32, BF16 = jnp.float32, jnp.bfloat16
PARAMS = pltpu.CompilerParams(vmem_limit_bytes=32 * 1024 * 1024)
NN = (((1,), (0,)), ((), ()))
NT = (((1,), (1,)), ((), ()))


def dot(a, b, dims=NN):
    return lax.dot_general(a, b, dims, preferred_element_type=F32)


def low_lanes(shape):
    return lax.broadcasted_iota(jnp.int32, shape, 1) < 64


def pick_matrix():
    row = lax.broadcasted_iota(jnp.int32, (256, 128), 0)
    col = lax.broadcasted_iota(jnp.int32, (256, 128), 1)
    return (2 * (row % 64) - 1 + row // 64 == col).astype(F32).astype(BF16)


def twice():
    row = lax.broadcasted_iota(jnp.int32, (64, 128), 0)
    col = lax.broadcasted_iota(jnp.int32, (64, 128), 1)
    return (row == col % 64).astype(F32).astype(BF16)


def gather_taps(plane, out):
    picked = dot(pick_matrix(), plane, NT).astype(BF16)
    low = low_lanes((64, 128))
    zero = jnp.zeros((64, 128), BF16)
    for y in range(8):
        for tz in range(4):
            block = picked[tz * 64 : tz * 64 + 64]
            above = block[:, y * 128 - 128 : y * 128] if y > 0 else zero
            below = block[:, y * 128 + 128 : y * 128 + 256] if y < 7 else zero
            rows = slice(y * 64, y * 64 + 64)
            out[rows, tz * 128 : tz * 128 + 128] = block[:, y * 128 : y * 128 + 128]
            out[rows, 512 + tz * 128 : 640 + tz * 128] = jnp.where(low, below, above)


def gather_coarse(field, out):
    row = lax.broadcasted_iota(jnp.int32, (512, 128), 0) % 64
    low = low_lanes((512, 128))
    before = jnp.where(row == 0, 0.0, pltpu.roll(field, 1, 0))
    after = jnp.where(row == 63, 0.0, pltpu.roll(field, 511, 0))
    sides = jnp.where(low, before, after).astype(BF16)
    mid = field.astype(BF16)
    zero = jnp.zeros((64, 128), BF16)
    up = jnp.concatenate([zero, mid[:448]], 0)
    down = jnp.concatenate([mid[64:], zero], 0)
    out[0:64, 0:128] = zero
    out[64:512, 0:128] = sides[:448]
    out[:, 128:256] = sides
    out[0:448, 256:384] = sides[64:]
    out[448:512, 256:384] = zero
    out[:, 384:512] = jnp.where(low, up, down)
    out[:, 512:640] = mid


def turned(ref):
    field = ref.astype(F32)
    return field, pltpu.roll(field, 64, 1)


def doubled(ref):
    field, swapped = turned(ref)
    low = low_lanes((256, 128))
    return jnp.concatenate([jnp.where(low, field, swapped), jnp.where(low, swapped, field)], 0)


def edges_kernel(volumes, cot, first, last, raw, raw_cot, planes, rows, sems):
    copies = [pltpu.make_async_copy(volumes.at[:, x], raw.at[x], sems.at[x]) for x in range(2)]
    copies.append(pltpu.make_async_copy(cot, raw_cot, sems.at[2]))
    for copy in copies:
        copy.start()
    for x, out in enumerate((first, last)):
        copies[x].wait()
        planes[x] = raw[x].astype(F32).reshape(1024, 128)
        for y in range(16):
            out[y * 64 : y * 64 + 64] = planes[x, pl.ds(y, 64, stride=16), :].astype(BF16)
    copies[2].wait()
    rows[...] = raw_cot[...].astype(F32).reshape(512, 64)
    for j in range(4):
        both = jnp.concatenate(
            [rows[pl.ds(j, 64, stride=8), :], rows[pl.ds(j + 4, 64, stride=8), :]], 0
        )
        block = both.T.astype(BF16)
        for out in (first, last):
            out[1024 + j * 64 : 1088 + j * 64] = block


def prepare_kernel(
    first, last, far_first, far_down, part, fw, dw, taps, w_first, w_down, sems
):
    weights = ((far_first, w_first), (far_down, w_down))
    copies = [pltpu.make_async_copy(far, to, sems.at[i]) for i, (far, to) in enumerate(weights)]
    for copy in copies:
        copy.start()
    low = low_lanes((64, 128))
    zero = jnp.zeros((64, 128), BF16)
    pair = twice()

    def both(ref, k):
        return dot(ref[k * 64 : k * 64 + 64], pair).astype(BF16)

    for x, ref in enumerate((first, last)):
        gather_taps(ref[0:1024], taps.at[:, x * 1024 : x * 1024 + 1024])
    for copy in copies:
        copy.wait()
    for dx in range(3):
        for tz in range(4):
            for qz in range(2):
                iz = tz - qz
                w = [both(w_first, dx * 9 + iy * 3 + iz) for iy in range(3)] if 0 <= iz < 3 else None
                for side in range(2):
                    at = dx * 1024 + side * 512 + tz * 128
                    lanes = slice(qz * 128, qz * 128 + 128)
                    if w is None:
                        upper = lower = zero
                    elif side == 0:
                        upper = jnp.where(low, w[1], w[0])
                        lower = jnp.where(low, w[2], w[1])
                    else:
                        upper = jnp.where(low, zero, w[2])
                        lower = jnp.where(low, w[0], zero)
                    fw[at : at + 64, lanes] = upper
                    fw[at + 64 : at + 128, lanes] = lower
    for x in range(2):
        for qz in range(2):
            for qy in range(2):
                k = x * 4 + qy * 2 + qz
                at = (x * 4 + qz * 2 + qy) * 64
                dw[at : at + 64] = both(w_down, k)
    for x in range(2):
        part[x * 512 : x * 512 + 512] = dot(taps[...], fw[1024 - x * 1024 : 3072 - x * 1024])


def first_kernel(before, after, part, fw, dw, act, pre, send, taps):
    low = low_lanes((256, 128))
    for x, side in enumerate((before, after)):
        gather_taps(side[0:1024], taps)
        value = part[x * 512 : x * 512 + 512] + dot(taps[...], fw[x * 2048 : x * 2048 + 1024])
        pre[x * 512 : x * 512 + 512] = value
        act[:, x * 256 : x * 256 + 256] = (value * jax.nn.sigmoid(value)).astype(BF16)
    down = dot(act[...], dw[...])
    send[...] = jnp.where(low, down[:256], down[256:]).astype(BF16)


def beside_kernel(
    first, before, after, pre, down, far_coarse, cw, bw, slope, ct, own, acc, w_coarse, sem
):
    copy = pltpu.make_async_copy(far_coarse, w_coarse, sem)
    copy.start()
    value = pre[...]
    s = jax.nn.sigmoid(value)
    slope[...] = s * (1.0 + value * (1.0 - s))
    low = low_lanes((256, 128))
    f0, t0 = turned(before[1024:1280])
    f1, t1 = turned(first[1024:1280])
    f2, t2 = turned(after[1024:1280])
    ct[0:256, 0:128] = jnp.where(low, f0, t1)
    ct[256:512, 0:128] = jnp.where(low, t0, f1)
    ct[0:256, 128:256] = f2
    ct[256:512, 128:256] = t2
    gather_coarse(doubled(down[...]), own)
    low = low_lanes((64, 128))
    zero = jnp.zeros((64, 128), BF16)
    pair = twice()

    def both(ref, k):
        return dot(ref[k * 64 : k * 64 + 64], pair).astype(BF16)

    copy.wait()
    order = [(0, 0), (0, 2), (1, 0), (1, 2), (2, 0), (2, 2), (0, 1), (2, 1), (1, 1), None]
    for j, tap in enumerate(order):
        if tap is None:
            w = [zero] * 3
        else:
            w = [both(w_coarse, dx * 9 + tap[0] * 3 + tap[1]) for dx in range(3)]
        w = [zero] * 2 + w + [zero] * 2
        for p in range(5):
            at = p * 640 + j * 64
            cw[at : at + 64, 0:128] = jnp.where(low, w[p + 2], w[p + 1])
            cw[at : at + 64, 128:256] = jnp.where(low, w[p], zero)
    for dx in range(3):
        back = [
            zero if tap is None else both(w_coarse, (2 - dx) * 9 + (2 - tap[0]) * 3 + 2 - tap[1])
            for tap in order
        ]
        for j in range(5):
            at = dx * 640 + j * 128
            bw[:, at : at + 128] = jnp.where(low, back[2 * j], back[2 * j + 1])
    acc[...] = dot(own[...], cw[1280:1920])


def rest_kernel(
    core, d0, d1, d3, d4, first, last, before, after, act, slope, ct, own, acc, dw, cw, bw, out, keep, send,
    grads, below, above, near, taps,
):
    low = low_lanes((64, 128))
    for p, ref in enumerate((before, first, last, after)):
        gather_taps(ref[0:1024], taps.at[p * 512 : p * 512 + 512])
    for p, ref in enumerate((d0, d1)):
        gather_coarse(doubled(ref[...]), below.at[:, p * 640 : p * 640 + 640])
    for p, ref in enumerate((d3, d4)):
        gather_coarse(doubled(ref[...]), above.at[:, p * 640 : p * 640 + 640])
    pre = acc[...] + dot(below[...], cw[0:1280]) + dot(above[...], cw[1920:3200])
    s = jax.nn.sigmoid(pre)
    out[...] = (pre[:, 0:128] * s[:, 0:128]).T[64:128].astype(BF16)
    grad = (ct[...] * (s * (1.0 + pre * (1.0 - s)))).astype(BF16).astype(F32)
    two, one = grad[:, 0:128], grad[:, 128:256]
    two_t, one_t = pltpu.roll(two, 64, 1), pltpu.roll(one, 64, 1)
    low2 = low_lanes((512, 128))
    gather_coarse(jnp.where(low2, two, two_t), near.at[:, 0:640])
    gather_coarse(jnp.where(low2, two_t, two), near.at[:, 640:1280])
    gather_coarse(jnp.where(low2, one, one_t), near.at[:, 1280:1920])
    dg_wide = dot(near[...], bw[...], NT)
    dg = dg_wide.astype(BF16)
    up = dot(dg, dw[:, 0:64], NT)
    fg_t = jnp.concatenate(
        [
            (up[:, x * 256 : x * 256 + 256] * slope[x * 512 : x * 512 + 512]).T.astype(BF16)
            for x in range(2)
        ],
        1,
    )
    mid_t = two.T[64:128].astype(BF16)
    center = []
    for dx, planes in enumerate((below[:, 640:1280], own[...], above[:, 0:640])):
        g = dot(mid_t, planes)
        for j in range(4):
            at = (14 + dx * 4 + j) * 64
            grads[at : at + 64] = g[:, j * 128 : j * 128 + 128].astype(BF16)
        center.append(g[:, 512:640])
    grads[26 * 64 : 27 * 64] = jnp.where(low, center[0], center[1]).astype(BF16)
    grads[27 * 64 : 28 * 64] = center[2].astype(BF16)
    gd = dot(dg_wide.T.astype(BF16), act[...])
    for j in range(4):
        at = (28 + j) * 64
        grads[at : at + 64] = gd[:, j * 128 : j * 128 + 128].astype(BF16)
    zero_y = []
    for dx in range(3):
        g = dot(fg_t, taps[dx * 512 : dx * 512 + 1024])
        for iz in range(3):

            def summed(side, qy):
                at = side * 512 + iz * 128
                return (
                    g[qy * 64 : qy * 64 + 64, at : at + 128]
                    + g[128 + qy * 64 : 192 + qy * 64, at + 128 : at + 256]
                )

            z0, z1, u0, u1 = summed(0, 0), summed(0, 1), summed(1, 0), summed(1, 1)
            j = dx * 3 + iz
            grads[j * 64 : j * 64 + 64] = (
                z0 + pltpu.roll(jnp.where(low, u1, z1), 64, 1)
            ).astype(BF16)
            zero_y.append((z1, u0))
    zero_y.append((jnp.zeros((64, 128), F32),) * 2)
    for m in range(5):
        (z1a, u0a), (z1b, u0b) = zero_y[2 * m], zero_y[2 * m + 1]
        at = (9 + m) * 64
        grads[at : at + 64] = (
            jnp.where(low, z1a, u0b) + pltpu.roll(jnp.where(low, z1b, u0a), 64, 1)
        ).astype(BF16)
    here = pl.multiple_of(core[0] * 1024, 1024)
    keep[...] = grads[pl.ds(here, 1024), :]
    send[...] = grads[pl.ds(pl.multiple_of(1024 - here, 1024), 1024), :]


def unpack_kernel(core, mine, other, first, down, coarse, packed):
    here = pl.multiple_of(core[0] * 1024, 1024)
    packed[pl.ds(here, 1024), :] = mine[...]
    packed[pl.ds(pl.multiple_of(1024 - here, 1024), 1024), :] = other[...]

    def block(b):
        return packed[b * 64 : b * 64 + 64].astype(F32).T

    for j in range(9):
        dx, iz = j // 3, j % 3
        t = block(j)
        first[dx, 1, iz] = t[0:64]
        first[dx, 2, iz] = t[64:128]
    for m in range(5):
        t = block(9 + m)
        for h in range(2):
            j = 2 * m + h
            if j < 9:
                first[j // 3, 0, j % 3] = t[h * 64 : h * 64 + 64]
    pairs = [((0, 0), (0, 2)), ((1, 0), (1, 2)), ((2, 0), (2, 2)), ((0, 1), (2, 1))]
    for dx in range(3):
        for j in range(4):
            t = block(14 + dx * 4 + j)
            for h in range(2):
                dy, dz = pairs[j][h]
                coarse[dx, dy, dz] = t[h * 64 : h * 64 + 64]
    t = block(26)
    coarse[0, 1, 1] = t[0:64]
    coarse[1, 1, 1] = t[64:128]
    coarse[2, 1, 1] = block(27)[0:64]
    for j in range(4):
        t = block(28 + j)
        for qy in range(2):
            down[j // 2, qy, j % 2] = t[qy * 64 : qy * 64 + 64]


def call(kernel, outs, scratch=(), places=""):
    kinds = {"s": pltpu.SMEM, "h": pltpu.HBM, "v": pltpu.VMEM}
    specs = {"in_specs": [pl.BlockSpec(memory_space=kinds[p]) for p in places]} if places else {}
    return pl.pallas_call(
        kernel,
        out_shape=[jax.ShapeDtypeStruct(s, d) for s, d in outs],
        scratch_shapes=[pltpu.VMEM(*s) if isinstance(s, tuple) else s for s in scratch],
        compiler_params=PARAMS,
        **specs,
    )


def far(value):
    return pltpu.with_memory_space_constraint(value, pltpu.HBM)


def scatter_sum(y, axis, count, groups=None):
    y = y.reshape(count, y.shape[0] // count, 128)
    y = lax.all_to_all(y, axis, 0, 0, tiled=True, axis_index_groups=groups)
    return jnp.sum(y.astype(F32), 0).astype(BF16)


def spread(y, axis, count, groups=None):
    y = jnp.broadcast_to(y[None], (count,) + y.shape)
    return lax.all_to_all(y, axis, 0, 0, tiled=True, axis_index_groups=groups)


def local(volumes, w_first, w_down, w_coarse, cotangent):
    n, m = lax.axis_size("space"), lax.axis_size("dp")

    def shift(value, by):
        steps = [(i, i + by) for i in range(n) if 0 <= i + by < n]
        return lax.ppermute(value, "space", steps)

    def partner(value):
        return lax.ppermute(value, "space", [(i, i ^ 1) for i in range(n)])

    first, last = call(
        edges_kernel,
        [((1280, 128), BF16)] * 2,
        [
            ((2, 64, 16, 128), BF16),
            ((64, 8, 64), BF16),
            ((2, 1024, 128), F32),
            ((512, 64), F32),
            pltpu.SemaphoreType.DMA((3,)),
        ],
        "hh",
    )(far(volumes.reshape(64, 2, 16, 128)), far(cotangent.reshape(64, 8, 64)))
    before = shift(last, 1)
    after = shift(first, -1)
    part, fw, dw = call(
        prepare_kernel,
        [((1024, 256), F32), ((3072, 256), BF16), ((512, 128), BF16)],
        [((512, 2048), BF16), ((1728, 64), BF16), ((512, 64), BF16), pltpu.SemaphoreType.DMA((2,))],
        "vvhh",
    )(first, last, far(w_first.reshape(1728, 64)), far(w_down.reshape(512, 64)))
    act, pre, down = call(
        first_kernel,
        [((512, 512), BF16), ((1024, 256), F32), ((256, 128), BF16)],
        [((512, 1024), BF16)],
    )(before, after, part, fw, dw)
    halo = [shift(down, 2), shift(down, 1), shift(down, -1), shift(down, -2)]
    cw, bw, slope, ct, own, acc = call(
        beside_kernel,
        [
            ((3200, 256), BF16),
            ((64, 1920), BF16),
            ((1024, 256), F32),
            ((512, 256), F32),
            ((512, 640), BF16),
            ((512, 256), F32),
        ],
        [((1728, 64), BF16), pltpu.SemaphoreType.DMA],
        "vvvvvh",
    )(first, before, after, pre, down, far(w_coarse.reshape(1728, 64)))
    core = lax.rem(lax.axis_index("space"), 2).reshape(1)
    out, keep, send = call(
        rest_kernel,
        [((64, 512), BF16), ((1024, 128), BF16), ((1024, 128), BF16)],
        [
            ((2048, 128), BF16),
            ((512, 1280), BF16),
            ((512, 1280), BF16),
            ((512, 1920), BF16),
            ((2048, 1024), BF16),
        ],
        "s" + 16 * "v",
    )(core, *halo, first, last, before, after, act, slope, ct, own, acc, dw, cw, bw)
    half = (keep.astype(F32) + partner(send).astype(F32)).astype(BF16)
    chips = [list(range(c, n, 2)) for c in range(2)]
    piece = scatter_sum(half, "dp", m)
    piece = jnp.sum(spread(piece, "space", n // 2, chips).astype(F32), 0).astype(BF16)
    mine = spread(piece, "dp", m).reshape(1024, 128)
    grad_first, grad_down, grad_coarse = call(
        unpack_kernel,
        [((3, 3, 3, 64, 64), F32), ((2, 2, 2, 64, 64), F32), ((3, 3, 3, 64, 64), F32)],
        [((2048, 128), BF16)],
        "svv",
    )(core, mine, partner(mine))
    return (out.reshape(1, 64, 1, 8, 64), grad_first, grad_down, grad_coarse)


def solution(mesh):
    return jax.shard_map(
        local,
        mesh=mesh,
        in_specs=(
            P("dp", None, "space", None, None),
            P(),
            P(),
            P(),
            P("dp", None, "space", None, None),
        ),
        out_specs=(P("dp", None, "space", None, None), P(), P(), P()),
        check_vma=False,
    )
```

```python
import jax
import jax.numpy as jnp
from jax import lax
from jax.experimental import pallas as pl
from jax.experimental.pallas import tpu as pltpu
from jax.sharding import PartitionSpec as P

F32, BF16 = jnp.float32, jnp.bfloat16
PARAMS = pltpu.CompilerParams(vmem_limit_bytes=32 * 1024 * 1024)
NN = (((1,), (0,)), ((), ()))
NT = (((1,), (1,)), ((), ()))


def dot(a, b, dims=NN):
    return lax.dot_general(a, b, dims, preferred_element_type=F32)


def core():
    return lax.axis_index("space") % 2


def low_lanes(shape):
    return lax.broadcasted_iota(jnp.int32, shape, 1) < 64


def pick_matrix():
    row = lax.broadcasted_iota(jnp.int32, (256, 128), 0)
    col = lax.broadcasted_iota(jnp.int32, (256, 128), 1)
    return (2 * (row % 64) - 1 + row // 64 == col).astype(F32).astype(BF16)


def twice():
    row = lax.broadcasted_iota(jnp.int32, (64, 128), 0)
    col = lax.broadcasted_iota(jnp.int32, (64, 128), 1)
    return (row == col % 64).astype(F32).astype(BF16)


def gather_taps(plane, out):
    picked = dot(pick_matrix(), plane, NT).astype(BF16)
    low = low_lanes((64, 128))
    zero = jnp.zeros((64, 128), BF16)
    for y in range(8):
        for tz in range(4):
            block = picked[tz * 64 : tz * 64 + 64]
            above = block[:, y * 128 - 128 : y * 128] if y > 0 else zero
            below = block[:, y * 128 + 128 : y * 128 + 256] if y < 7 else zero
            rows = slice(y * 64, y * 64 + 64)
            out[rows, tz * 128 : tz * 128 + 128] = block[:, y * 128 : y * 128 + 128]
            out[rows, 512 + tz * 128 : 640 + tz * 128] = jnp.where(low, below, above)


def gather_coarse(field, out):
    row = lax.broadcasted_iota(jnp.int32, (512, 128), 0) % 64
    low = low_lanes((512, 128))
    before = jnp.where(row == 0, 0.0, pltpu.roll(field, 1, 0))
    after = jnp.where(row == 63, 0.0, pltpu.roll(field, 511, 0))
    sides = jnp.where(low, before, after).astype(BF16)
    mid = field.astype(BF16)
    zero = jnp.zeros((64, 128), BF16)
    up = jnp.concatenate([zero, mid[:448]], 0)
    down = jnp.concatenate([mid[64:], zero], 0)
    out[0:64, 0:128] = zero
    out[64:512, 0:128] = sides[:448]
    out[:, 128:256] = sides
    out[0:448, 256:384] = sides[64:]
    out[448:512, 256:384] = zero
    out[:, 384:512] = jnp.where(low, up, down)
    out[:, 512:640] = mid


def turned(ref):
    field = ref.astype(F32)
    return field, pltpu.roll(field, 64, 1)


def doubled(ref):
    field, swapped = turned(ref)
    low = low_lanes((256, 128))
    return jnp.concatenate([jnp.where(low, field, swapped), jnp.where(low, swapped, field)], 0)


def edges_kernel(volumes, cot, first, last, inner, outer, raw, raw_cot, planes, rows, sems):
    copies = [pltpu.make_async_copy(volumes.at[:, x], raw.at[x], sems.at[x]) for x in range(2)]
    copies.append(pltpu.make_async_copy(cot, raw_cot, sems.at[2]))
    for copy in copies:
        copy.start()
    for x, out in enumerate((first, last)):
        copies[x].wait()
        planes[x] = raw[x].astype(F32).reshape(1024, 128)
        for y in range(16):
            out[y * 64 : y * 64 + 64] = planes[x, pl.ds(y, 64, stride=16), :].astype(BF16)
    copies[2].wait()
    rows[...] = raw_cot[...].astype(F32).reshape(512, 64)
    for j in range(4):
        both = jnp.concatenate(
            [rows[pl.ds(j, 64, stride=8), :], rows[pl.ds(j + 4, 64, stride=8), :]], 0
        )
        block = both.T.astype(BF16)
        for out in (first, last):
            out[1024 + j * 64 : 1088 + j * 64] = block
    even = core() == 0
    inner[...] = jnp.where(even, last[...], first[...])
    outer[...] = jnp.where(even, first[...], last[...])


def prepare_kernel(
    first, last, far_first, far_down, part, fw, dw, taps, w_first, w_down, sems
):
    weights = ((far_first, w_first), (far_down, w_down))
    copies = [pltpu.make_async_copy(far, to, sems.at[i]) for i, (far, to) in enumerate(weights)]
    for copy in copies:
        copy.start()
    low = low_lanes((64, 128))
    zero = jnp.zeros((64, 128), BF16)
    pair = twice()

    def both(ref, k):
        return dot(ref[k * 64 : k * 64 + 64], pair).astype(BF16)

    for x, ref in enumerate((first, last)):
        gather_taps(ref[0:1024], taps.at[:, x * 1024 : x * 1024 + 1024])
    for copy in copies:
        copy.wait()
    for dx in range(3):
        for iz in range(-1, 4):
            if 0 <= iz < 3:
                w = [both(w_first, dx * 9 + iy * 3 + iz) for iy in range(3)]
                blocks = (
                    (jnp.where(low, w[1], w[0]), jnp.where(low, w[2], w[1])),
                    (jnp.where(low, zero, w[2]), jnp.where(low, w[0], zero)),
                )
            else:
                blocks = ((zero, zero),) * 2
            for qz in range(2):
                tz = iz + qz
                for side in range(2 if 0 <= tz < 4 else 0):
                    at = dx * 1024 + side * 512 + tz * 128
                    for half in range(2):
                        rows = slice(at + half * 64, at + half * 64 + 64)
                        fw[rows, qz * 128 : qz * 128 + 128] = blocks[side][half]
    for x in range(2):
        for qz in range(2):
            for qy in range(2):
                k = x * 4 + qy * 2 + qz
                at = (x * 4 + qz * 2 + qy) * 64
                dw[at : at + 64] = both(w_down, k)
    for x in range(2):
        part[x * 512 : x * 512 + 512] = dot(taps[...], fw[1024 - x * 1024 : 3072 - x * 1024])


def first_kernel(outer, inner, part, fw, dw, act, pre, send, before, after, taps):
    low = low_lanes((256, 128))
    even = core() == 0
    before[...] = jnp.where(even, outer[...], inner[...])
    after[...] = jnp.where(even, inner[...], outer[...])
    for x, side in enumerate((before, after)):
        gather_taps(side[0:1024], taps)
        value = part[x * 512 : x * 512 + 512] + dot(taps[...], fw[x * 2048 : x * 2048 + 1024])
        pre[x * 512 : x * 512 + 512] = value
        act[:, x * 256 : x * 256 + 256] = (value * jax.nn.sigmoid(value)).astype(BF16)
    down = dot(act[...], dw[...])
    send[...] = jnp.where(low, down[:256], down[256:]).astype(BF16)


def beside_kernel(
    first, before, after, pre, down, far_coarse, cw, bw, slope, ct, own, acc, w_coarse, sem
):
    copy = pltpu.make_async_copy(far_coarse, w_coarse, sem)
    copy.start()
    value = pre[...]
    s = jax.nn.sigmoid(value)
    slope[...] = s * (1.0 + value * (1.0 - s))
    low = low_lanes((256, 128))
    f0, t0 = turned(before[1024:1280])
    f1, t1 = turned(first[1024:1280])
    f2, t2 = turned(after[1024:1280])
    ct[0:256, 0:128] = jnp.where(low, f0, t1)
    ct[256:512, 0:128] = jnp.where(low, t0, f1)
    ct[0:256, 128:256] = f2
    ct[256:512, 128:256] = t2
    gather_coarse(doubled(down[...]), own)
    low = low_lanes((64, 128))
    zero = jnp.zeros((64, 128), BF16)
    pair = twice()

    def both(ref, k):
        return dot(ref[k * 64 : k * 64 + 64], pair).astype(BF16)

    copy.wait()
    order = [(0, 0), (0, 2), (1, 0), (1, 2), (2, 0), (2, 2), (0, 1), (2, 1), (1, 1), None]
    for j, tap in enumerate(order):
        if tap is None:
            w = [zero] * 3
        else:
            w = [both(w_coarse, dx * 9 + tap[0] * 3 + tap[1]) for dx in range(3)]
        w = [zero] * 2 + w + [zero] * 2
        for p in range(5):
            at = p * 640 + j * 64
            cw[at : at + 64, 0:128] = jnp.where(low, w[p + 2], w[p + 1])
            cw[at : at + 64, 128:256] = jnp.where(low, w[p], zero)
    for dx in range(3):
        back = [
            zero if tap is None else both(w_coarse, (2 - dx) * 9 + (2 - tap[0]) * 3 + 2 - tap[1])
            for tap in order
        ]
        for j in range(5):
            at = dx * 640 + j * 128
            bw[:, at : at + 128] = jnp.where(low, back[2 * j], back[2 * j + 1])
    acc[...] = dot(own[...], cw[1280:1920])


def rest_kernel(
    outer, chips1, chips0, inner, first, last, before, after, act, slope, ct, own, acc, dw, cw, bw, out, keep, send,
    grads, below, above, near, taps,
):
    low = low_lanes((64, 128))
    for p, ref in enumerate((before, first, last, after)):
        gather_taps(ref[0:1024], taps.at[p * 512 : p * 512 + 512])
    even, even_chip = core() == 0, lax.axis_index("space") // 2 % 2 == 0
    i, o, a, b = inner[...], outer[...], chips0[...], chips1[...]
    for p, plane in enumerate((jnp.where(even_chip, b, a), jnp.where(even, o, i))):
        gather_coarse(doubled(plane), below.at[:, p * 640 : p * 640 + 640])
    for p, plane in enumerate((jnp.where(even, i, o), jnp.where(even_chip, a, b))):
        gather_coarse(doubled(plane), above.at[:, p * 640 : p * 640 + 640])
    pre = acc[...] + dot(below[...], cw[0:1280]) + dot(above[...], cw[1920:3200])
    s = jax.nn.sigmoid(pre)
    out[...] = (pre[:, 0:128] * s[:, 0:128]).T[64:128].astype(BF16)
    grad = (ct[...] * (s * (1.0 + pre * (1.0 - s)))).astype(BF16).astype(F32)
    two, one = grad[:, 0:128], grad[:, 128:256]
    two_t, one_t = pltpu.roll(two, 64, 1), pltpu.roll(one, 64, 1)
    low2 = low_lanes((512, 128))
    gather_coarse(jnp.where(low2, two, two_t), near.at[:, 0:640])
    gather_coarse(jnp.where(low2, two_t, two), near.at[:, 640:1280])
    gather_coarse(jnp.where(low2, one, one_t), near.at[:, 1280:1920])
    dg_wide = dot(near[...], bw[...], NT)
    dg = dg_wide.astype(BF16)
    up = dot(dg, dw[:, 0:64], NT)
    fg_t = jnp.concatenate(
        [
            (up[:, x * 256 : x * 256 + 256] * slope[x * 512 : x * 512 + 512]).T.astype(BF16)
            for x in range(2)
        ],
        1,
    )
    mid_t = two.T[64:128].astype(BF16)
    center = []
    for dx, planes in enumerate((below[:, 640:1280], own[...], above[:, 0:640])):
        g = dot(mid_t, planes)
        for j in range(4):
            at = (14 + dx * 4 + j) * 64
            grads[at : at + 64] = g[:, j * 128 : j * 128 + 128].astype(BF16)
        center.append(g[:, 512:640])
    grads[26 * 64 : 27 * 64] = jnp.where(low, center[0], center[1]).astype(BF16)
    grads[27 * 64 : 28 * 64] = center[2].astype(BF16)
    gd = dot(dg_wide.T.astype(BF16), act[...])
    for j in range(4):
        at = (28 + j) * 64
        grads[at : at + 64] = gd[:, j * 128 : j * 128 + 128].astype(BF16)
    zero_y = []
    for dx in range(3):
        g = dot(fg_t, taps[dx * 512 : dx * 512 + 1024])
        for iz in range(3):

            def summed(side, qy):
                at = side * 512 + iz * 128
                return (
                    g[qy * 64 : qy * 64 + 64, at : at + 128]
                    + g[128 + qy * 64 : 192 + qy * 64, at + 128 : at + 256]
                )

            z0, z1, u0, u1 = summed(0, 0), summed(0, 1), summed(1, 0), summed(1, 1)
            j = dx * 3 + iz
            grads[j * 64 : j * 64 + 64] = (
                z0 + pltpu.roll(jnp.where(low, u1, z1), 64, 1)
            ).astype(BF16)
            zero_y.append((z1, u0))
    zero_y.append((jnp.zeros((64, 128), F32),) * 2)
    for m in range(5):
        (z1a, u0a), (z1b, u0b) = zero_y[2 * m], zero_y[2 * m + 1]
        at = (9 + m) * 64
        grads[at : at + 64] = (
            jnp.where(low, z1a, u0b) + pltpu.roll(jnp.where(low, z1b, u0a), 64, 1)
        ).astype(BF16)
    here = pl.multiple_of(core() * 1024, 1024)
    keep[...] = grads[pl.ds(here, 1024), :]
    send[...] = grads[pl.ds(pl.multiple_of(1024 - here, 1024), 1024), :]


def unpack_kernel(mine, other, far_first, far_down, far_coarse, packed, first, down, coarse, sems):
    here = pl.multiple_of(core() * 1024, 1024)
    packed[pl.ds(here, 1024), :] = mine[...]
    packed[pl.ds(pl.multiple_of(1024 - here, 1024), 1024), :] = other[...]
    copies = []

    def send(value, far):
        copies.append(pltpu.make_async_copy(value, far, sems.at[len(copies)]))
        copies[-1].start()

    def block(b):
        return packed[b * 64 : b * 64 + 64].astype(F32).T

    pairs = [((0, 0), (0, 2)), ((1, 0), (1, 2)), ((2, 0), (2, 2)), ((0, 1), (2, 1))]
    t, u = block(26), block(27)
    centers = (t[0:64], t[64:128], u[0:64])
    for dx in range(3):
        coarse[dx, 1, 1] = centers[dx]
        for j in range(4):
            t = block(14 + dx * 4 + j)
            for h in range(2):
                dy, dz = pairs[j][h]
                coarse[dx, dy, dz] = t[h * 64 : h * 64 + 64]
        send(coarse.at[dx], far_coarse.at[dx])
    for m in range(5):
        t = block(9 + m)
        for h in range(2):
            j = 2 * m + h
            if j < 9:
                first[j // 3, 0, j % 3] = t[h * 64 : h * 64 + 64]
    for dx in range(3):
        for iz in range(3):
            t = block(dx * 3 + iz)
            first[dx, 1, iz] = t[0:64]
            first[dx, 2, iz] = t[64:128]
        send(first.at[dx], far_first.at[dx])
    for j in range(4):
        t = block(28 + j)
        for qy in range(2):
            down[j // 2, qy, j % 2] = t[qy * 64 : qy * 64 + 64]
    send(down, far_down)
    for copy in copies:
        copy.wait()


def call(kernel, outs, scratch=(), places="", home=""):
    kinds = {"h": pltpu.HBM, "v": pltpu.VMEM}
    specs = {"in_specs": [pl.BlockSpec(memory_space=kinds[p]) for p in places]} if places else {}
    if home:
        specs["out_specs"] = [pl.BlockSpec(memory_space=kinds[p]) for p in home]
    return pl.pallas_call(
        kernel,
        out_shape=[jax.ShapeDtypeStruct(s, d) for s, d in outs],
        scratch_shapes=[pltpu.VMEM(*s) if isinstance(s, tuple) else s for s in scratch],
        compiler_params=PARAMS,
        **specs,
    )


def far(value):
    return pltpu.with_memory_space_constraint(value, pltpu.HBM)


def scatter_sum(y, axis, count, groups=None):
    y = y.reshape(count, y.shape[0] // count, 128)
    y = lax.all_to_all(y, axis, 0, 0, tiled=True, axis_index_groups=groups)
    return jnp.sum(y.astype(F32), 0).astype(BF16)


def spread(y, axis, count, groups=None):
    y = jnp.broadcast_to(y[None], (count,) + y.shape)
    return lax.all_to_all(y, axis, 0, 0, tiled=True, axis_index_groups=groups)


def local(volumes, w_first, w_down, w_coarse, cotangent):
    n, m = lax.axis_size("space"), lax.axis_size("dp")

    def swap(value, pairs):
        return lax.ppermute(value, "space", [p for i, j in pairs for p in ((i, j), (j, i))])

    chip = [(i, i + 1) for i in range(0, n, 2)]
    across = [(i, i + 1) for i in range(1, n - 1, 2)]
    beside = [[(i, i + 2) for i in range(n - 2) if i // 2 % 2 == k] for k in range(2)]
    first, last, inner, outer = call(
        edges_kernel,
        [((1280, 128), BF16)] * 4,
        [
            ((2, 64, 16, 128), BF16),
            ((64, 8, 64), BF16),
            ((2, 1024, 128), F32),
            ((512, 64), F32),
            pltpu.SemaphoreType.DMA((3,)),
        ],
        "hh",
    )(far(volumes.reshape(64, 2, 16, 128)), far(cotangent.reshape(64, 8, 64)))
    inner, outer = swap(inner, chip), swap(outer, across)
    part, fw, dw = call(
        prepare_kernel,
        [((1024, 256), F32), ((3072, 256), BF16), ((512, 128), BF16)],
        [((512, 2048), BF16), ((1728, 64), BF16), ((512, 64), BF16), pltpu.SemaphoreType.DMA((2,))],
        "vvhh",
    )(first, last, far(w_first.reshape(1728, 64)), far(w_down.reshape(512, 64)))
    act, pre, down, before, after = call(
        first_kernel,
        [((512, 512), BF16), ((1024, 256), F32), ((256, 128), BF16)] + [((1280, 128), BF16)] * 2,
        [((512, 1024), BF16)],
        "vvvvv",
    )(outer, inner, part, fw, dw)
    halo = [swap(down, pairs) for pairs in (across, beside[1], beside[0], chip)]
    cw, bw, slope, ct, own, acc = call(
        beside_kernel,
        [
            ((3200, 256), BF16),
            ((64, 1920), BF16),
            ((1024, 256), F32),
            ((512, 256), F32),
            ((512, 640), BF16),
            ((512, 256), F32),
        ],
        [((1728, 64), BF16), pltpu.SemaphoreType.DMA],
        "vvvvvh",
    )(first, before, after, pre, down, far(w_coarse.reshape(1728, 64)))
    out, keep, send = call(
        rest_kernel,
        [((64, 512), BF16), ((1024, 128), BF16), ((1024, 128), BF16)],
        [
            ((2048, 128), BF16),
            ((512, 1280), BF16),
            ((512, 1280), BF16),
            ((512, 1920), BF16),
            ((2048, 1024), BF16),
        ],
        16 * "v",
    )(*halo, first, last, before, after, act, slope, ct, own, acc, dw, cw, bw)
    half = (keep.astype(F32) + swap(send, chip).astype(F32)).astype(BF16)
    chips = [list(range(c, n, 2)) for c in range(2)]
    piece = scatter_sum(half, "dp", m)
    piece = jnp.sum(spread(piece, "space", n // 2, chips).astype(F32), 0).astype(BF16)
    mine = spread(piece, "dp", m).reshape(1024, 128)
    grad_first, grad_down, grad_coarse = call(
        unpack_kernel,
        [((3, 3, 3, 64, 64), F32), ((2, 2, 2, 64, 64), F32), ((3, 3, 3, 64, 64), F32)],
        [
            ((2048, 128), BF16),
            ((3, 3, 3, 64, 64), F32),
            ((2, 2, 2, 64, 64), F32),
            ((3, 3, 3, 64, 64), F32),
            pltpu.SemaphoreType.DMA((7,)),
        ],
        "vv",
        "hhh",
    )(mine, swap(mine, chip))
    return (out.reshape(1, 64, 1, 8, 64), grad_first, grad_down, grad_coarse)


def solution(mesh):
    return jax.shard_map(
        local,
        mesh=mesh,
        in_specs=(
            P("dp", None, "space", None, None),
            P(),
            P(),
            P(),
            P("dp", None, "space", None, None),
        ),
        out_specs=(P("dp", None, "space", None, None), P(), P(), P()),
        check_vma=False,
    )
```

```python
import jax
import jax.numpy as jnp
from jax import lax
from jax.experimental import pallas as pl
from jax.experimental.pallas import tpu as pltpu
from jax.sharding import PartitionSpec as P

F32, BF16 = jnp.float32, jnp.bfloat16
PARAMS = pltpu.CompilerParams(vmem_limit_bytes=32 * 1024 * 1024)
NN = (((1,), (0,)), ((), ()))
NT = (((1,), (1,)), ((), ()))


def dot(a, b, dims=NN):
    return lax.dot_general(a, b, dims, preferred_element_type=F32)


def core():
    return lax.axis_index("space") % 2


def low_lanes(shape):
    return lax.broadcasted_iota(jnp.int32, shape, 1) < 64


def pick_matrix():
    row = lax.broadcasted_iota(jnp.int32, (256, 128), 0)
    col = lax.broadcasted_iota(jnp.int32, (256, 128), 1)
    return (2 * (row % 64) - 1 + row // 64 == col).astype(F32).astype(BF16)


def twice():
    row = lax.broadcasted_iota(jnp.int32, (64, 128), 0)
    col = lax.broadcasted_iota(jnp.int32, (64, 128), 1)
    return (row == col % 64).astype(F32).astype(BF16)


def gather_taps(plane, out):
    picked = dot(pick_matrix(), plane, NT).astype(BF16)
    low = low_lanes((64, 128))
    zero = jnp.zeros((64, 128), BF16)
    for y in range(8):
        for tz in range(4):
            block = picked[tz * 64 : tz * 64 + 64]
            above = block[:, y * 128 - 128 : y * 128] if y > 0 else zero
            below = block[:, y * 128 + 128 : y * 128 + 256] if y < 7 else zero
            rows = slice(y * 64, y * 64 + 64)
            out[rows, tz * 128 : tz * 128 + 128] = block[:, y * 128 : y * 128 + 128]
            out[rows, 512 + tz * 128 : 640 + tz * 128] = jnp.where(low, below, above)


def gather_coarse(field, out):
    row = lax.broadcasted_iota(jnp.int32, (512, 128), 0) % 64
    low = low_lanes((512, 128))
    before = jnp.where(row == 0, 0.0, pltpu.roll(field, 1, 0))
    after = jnp.where(row == 63, 0.0, pltpu.roll(field, 511, 0))
    sides = jnp.where(low, before, after).astype(BF16)
    mid = field.astype(BF16)
    zero = jnp.zeros((64, 128), BF16)
    up = jnp.concatenate([zero, mid[:448]], 0)
    down = jnp.concatenate([mid[64:], zero], 0)
    out[0:64, 0:128] = zero
    out[64:512, 0:128] = sides[:448]
    out[:, 128:256] = sides
    out[0:448, 256:384] = sides[64:]
    out[448:512, 256:384] = zero
    out[:, 384:512] = jnp.where(low, up, down)
    out[:, 512:640] = mid


def turned(ref):
    field = ref.astype(F32)
    return field, pltpu.roll(field, 64, 1)


def doubled(ref):
    field, swapped = turned(ref)
    low = low_lanes((256, 128))
    return jnp.concatenate([jnp.where(low, field, swapped), jnp.where(low, swapped, field)], 0)


def edges_kernel(volumes, cot, first, last, inner, outer, raw, raw_cot, planes, rows, sems):
    copies = [pltpu.make_async_copy(volumes.at[:, x], raw.at[x], sems.at[x]) for x in range(2)]
    copies.append(pltpu.make_async_copy(cot, raw_cot, sems.at[2]))
    for copy in copies:
        copy.start()
    for x, out in enumerate((first, last)):
        copies[x].wait()
        planes[x] = raw[x].astype(F32).reshape(1024, 128)
        for y in range(16):
            out[y * 64 : y * 64 + 64] = planes[x, pl.ds(y, 64, stride=16), :].astype(BF16)
    copies[2].wait()
    rows[...] = raw_cot[...].astype(F32).reshape(512, 64)
    for j in range(4):
        both = jnp.concatenate(
            [rows[pl.ds(j, 64, stride=8), :], rows[pl.ds(j + 4, 64, stride=8), :]], 0
        )
        block = both.T.astype(BF16)
        for out in (first, last):
            out[1024 + j * 64 : 1088 + j * 64] = block
    even = core() == 0
    inner[...] = jnp.where(even, last[...], first[...])
    outer[...] = jnp.where(even, first[...], last[...])


def prepare_kernel(
    first, last, far_first, far_down, part, fw, dw, taps, w_first, w_down, wide_first, wide_down, sems
):
    weights = ((far_first, w_first), (far_down, w_down))
    copies = [pltpu.make_async_copy(far, to, sems.at[i]) for i, (far, to) in enumerate(weights)]
    for copy in copies:
        copy.start()
    low = low_lanes((64, 128))
    zero = jnp.zeros((64, 128), BF16)
    pair = twice()

    def both(ref, k):
        return ref[k * 64 : k * 64 + 64]

    for x, ref in enumerate((first, last)):
        gather_taps(ref[0:1024], taps.at[:, x * 1024 : x * 1024 + 1024])
    for copy in copies:
        copy.wait()
    wide_first[...] = dot(w_first[...], pair).astype(BF16)
    wide_down[...] = dot(w_down[...], pair).astype(BF16)
    for dx in range(3):
        for iz in range(-1, 4):
            if 0 <= iz < 3:
                w = [both(wide_first, dx * 9 + iy * 3 + iz) for iy in range(3)]
                blocks = (
                    (jnp.where(low, w[1], w[0]), jnp.where(low, w[2], w[1])),
                    (jnp.where(low, zero, w[2]), jnp.where(low, w[0], zero)),
                )
            else:
                blocks = ((zero, zero),) * 2
            for qz in range(2):
                tz = iz + qz
                for side in range(2 if 0 <= tz < 4 else 0):
                    at = dx * 1024 + side * 512 + tz * 128
                    for half in range(2):
                        rows = slice(at + half * 64, at + half * 64 + 64)
                        fw[rows, qz * 128 : qz * 128 + 128] = blocks[side][half]
    for x in range(2):
        for qz in range(2):
            for qy in range(2):
                k = x * 4 + qy * 2 + qz
                at = (x * 4 + qz * 2 + qy) * 64
                dw[at : at + 64] = both(wide_down, k)
    for x in range(2):
        part[x * 512 : x * 512 + 512] = dot(taps[...], fw[1024 - x * 1024 : 3072 - x * 1024])


def first_kernel(outer, inner, part, fw, dw, act, slope, send, before, after, taps):
    low = low_lanes((256, 128))
    even = core() == 0
    before[...] = jnp.where(even, outer[...], inner[...])
    after[...] = jnp.where(even, inner[...], outer[...])
    for x, side in enumerate((before, after)):
        gather_taps(side[0:1024], taps)
        value = part[x * 512 : x * 512 + 512] + dot(taps[...], fw[x * 2048 : x * 2048 + 1024])
        s = jax.nn.sigmoid(value)
        slope[x * 512 : x * 512 + 512] = s * (1.0 + value * (1.0 - s))
        act[:, x * 256 : x * 256 + 256] = (value * s).astype(BF16)
    down = dot(act[...], dw[...])
    send[...] = jnp.where(low, down[:256], down[256:]).astype(BF16)


def beside_kernel(
    first, before, after, down, far_coarse, cw, bw, ct, own, acc, w_coarse, wide, sem
):
    copy = pltpu.make_async_copy(far_coarse, w_coarse, sem)
    copy.start()
    low = low_lanes((256, 128))
    f0, t0 = turned(before[1024:1280])
    f1, t1 = turned(first[1024:1280])
    f2, t2 = turned(after[1024:1280])
    ct[0:256, 0:128] = jnp.where(low, f0, t1)
    ct[256:512, 0:128] = jnp.where(low, t0, f1)
    ct[0:256, 128:256] = f2
    ct[256:512, 128:256] = t2
    gather_coarse(doubled(down[...]), own)
    low = low_lanes((64, 128))
    zero = jnp.zeros((64, 128), BF16)
    pair = twice()

    def both(ref, k):
        return ref[k * 64 : k * 64 + 64]

    copy.wait()
    wide[...] = dot(w_coarse[...], pair).astype(BF16)
    order = [(0, 0), (0, 2), (1, 0), (1, 2), (2, 0), (2, 2), (0, 1), (2, 1), (1, 1), None]
    for j, tap in enumerate(order):
        if tap is None:
            w = [zero] * 3
        else:
            w = [both(wide, dx * 9 + tap[0] * 3 + tap[1]) for dx in range(3)]
        w = [zero] * 2 + w + [zero] * 2
        for p in range(5):
            at = p * 640 + j * 64
            cw[at : at + 64, 0:128] = jnp.where(low, w[p + 2], w[p + 1])
            cw[at : at + 64, 128:256] = jnp.where(low, w[p], zero)
    for dx in range(3):
        back = [
            zero if tap is None else both(wide, (2 - dx) * 9 + (2 - tap[0]) * 3 + 2 - tap[1])
            for tap in order
        ]
        for j in range(5):
            at = dx * 640 + j * 128
            bw[:, at : at + 128] = jnp.where(low, back[2 * j], back[2 * j + 1])
    acc[...] = dot(own[...], cw[1280:1920])


def rest_kernel(
    outer, chips1, chips0, inner, first, last, before, after, act, slope, ct, own, acc, dw, cw, bw, out, keep, send,
    grads, below, above, near, taps,
):
    low = low_lanes((64, 128))
    for p, ref in enumerate((before, first, last, after)):
        gather_taps(ref[0:1024], taps.at[p * 512 : p * 512 + 512])
    even, even_chip = core() == 0, lax.axis_index("space") // 2 % 2 == 0
    i, o, a, b = inner[...], outer[...], chips0[...], chips1[...]
    for p, plane in enumerate((jnp.where(even_chip, b, a), jnp.where(even, o, i))):
        gather_coarse(doubled(plane), below.at[:, p * 640 : p * 640 + 640])
    for p, plane in enumerate((jnp.where(even, i, o), jnp.where(even_chip, a, b))):
        gather_coarse(doubled(plane), above.at[:, p * 640 : p * 640 + 640])
    pre = acc[...] + dot(below[...], cw[0:1280]) + dot(above[...], cw[1920:3200])
    s = jax.nn.sigmoid(pre)
    out[...] = (pre[:, 0:128] * s[:, 0:128]).T[64:128].astype(BF16)
    grad = (ct[...] * (s * (1.0 + pre * (1.0 - s)))).astype(BF16).astype(F32)
    two, one = grad[:, 0:128], grad[:, 128:256]
    two_t, one_t = pltpu.roll(two, 64, 1), pltpu.roll(one, 64, 1)
    low2 = low_lanes((512, 128))
    gather_coarse(jnp.where(low2, two, two_t), near.at[:, 0:640])
    gather_coarse(jnp.where(low2, two_t, two), near.at[:, 640:1280])
    gather_coarse(jnp.where(low2, one, one_t), near.at[:, 1280:1920])
    dg_wide = dot(near[...], bw[...], NT)
    dg = dg_wide.astype(BF16)
    up = dot(dg, dw[:, 0:64], NT)
    fg_t = jnp.concatenate(
        [
            (up[:, x * 256 : x * 256 + 256] * slope[x * 512 : x * 512 + 512]).T.astype(BF16)
            for x in range(2)
        ],
        1,
    )
    mid_t = two.T[64:128].astype(BF16)
    center = []
    for dx, planes in enumerate((below[:, 640:1280], own[...], above[:, 0:640])):
        g = dot(mid_t, planes)
        for j in range(4):
            at = (14 + dx * 4 + j) * 64
            grads[at : at + 64] = g[:, j * 128 : j * 128 + 128].astype(BF16)
        center.append(g[:, 512:640])
    grads[26 * 64 : 27 * 64] = jnp.where(low, center[0], center[1]).astype(BF16)
    grads[27 * 64 : 28 * 64] = center[2].astype(BF16)
    gd = dot(dg_wide.T.astype(BF16), act[...])
    for j in range(4):
        at = (28 + j) * 64
        grads[at : at + 64] = gd[:, j * 128 : j * 128 + 128].astype(BF16)
    zero_y = []
    for dx in range(3):
        g = dot(fg_t, taps[dx * 512 : dx * 512 + 1024])
        for iz in range(3):

            def summed(side, qy):
                at = side * 512 + iz * 128
                return (
                    g[qy * 64 : qy * 64 + 64, at : at + 128]
                    + g[128 + qy * 64 : 192 + qy * 64, at + 128 : at + 256]
                )

            z0, z1, u0, u1 = summed(0, 0), summed(0, 1), summed(1, 0), summed(1, 1)
            j = dx * 3 + iz
            grads[j * 64 : j * 64 + 64] = (
                z0 + pltpu.roll(jnp.where(low, u1, z1), 64, 1)
            ).astype(BF16)
            zero_y.append((z1, u0))
    zero_y.append((jnp.zeros((64, 128), F32),) * 2)
    for m in range(5):
        (z1a, u0a), (z1b, u0b) = zero_y[2 * m], zero_y[2 * m + 1]
        at = (9 + m) * 64
        grads[at : at + 64] = (
            jnp.where(low, z1a, u0b) + pltpu.roll(jnp.where(low, z1b, u0a), 64, 1)
        ).astype(BF16)
    here = pl.multiple_of(core() * 1024, 1024)
    keep[...] = grads[pl.ds(here, 1024), :]
    send[...] = grads[pl.ds(pl.multiple_of(1024 - here, 1024), 1024), :]


def unpack_kernel(mine, other, far_first, far_down, far_coarse, packed, first, down, coarse, sems):
    here = pl.multiple_of(core() * 1024, 1024)
    packed[pl.ds(here, 1024), :] = mine[...]
    packed[pl.ds(pl.multiple_of(1024 - here, 1024), 1024), :] = other[...]
    copies = []

    def send(value, far):
        copies.append(pltpu.make_async_copy(value, far, sems.at[len(copies)]))
        copies[-1].start()

    def block(b):
        return packed[b * 64 : b * 64 + 64].astype(F32).T

    pairs = [((0, 0), (0, 2)), ((1, 0), (1, 2)), ((2, 0), (2, 2)), ((0, 1), (2, 1))]
    t, u = block(26), block(27)
    centers = (t[0:64], t[64:128], u[0:64])
    for dx in range(3):
        coarse[dx, 1, 1] = centers[dx]
        for j in range(4):
            t = block(14 + dx * 4 + j)
            for h in range(2):
                dy, dz = pairs[j][h]
                coarse[dx, dy, dz] = t[h * 64 : h * 64 + 64]
        send(coarse.at[dx], far_coarse.at[dx])
    for m in range(5):
        t = block(9 + m)
        for h in range(2):
            j = 2 * m + h
            if j < 9:
                first[j // 3, 0, j % 3] = t[h * 64 : h * 64 + 64]
    for dx in range(3):
        for iz in range(3):
            t = block(dx * 3 + iz)
            first[dx, 1, iz] = t[0:64]
            first[dx, 2, iz] = t[64:128]
        send(first.at[dx], far_first.at[dx])
    for j in range(4):
        t = block(28 + j)
        for qy in range(2):
            down[j // 2, qy, j % 2] = t[qy * 64 : qy * 64 + 64]
    send(down, far_down)
    for copy in copies:
        copy.wait()


def call(kernel, outs, scratch=(), places="", home=""):
    kinds = {"h": pltpu.HBM, "v": pltpu.VMEM}
    specs = {"in_specs": [pl.BlockSpec(memory_space=kinds[p]) for p in places]} if places else {}
    if home:
        specs["out_specs"] = [pl.BlockSpec(memory_space=kinds[p]) for p in home]
    return pl.pallas_call(
        kernel,
        out_shape=[jax.ShapeDtypeStruct(s, d) for s, d in outs],
        scratch_shapes=[pltpu.VMEM(*s) if isinstance(s, tuple) else s for s in scratch],
        compiler_params=PARAMS,
        **specs,
    )


def far(value):
    return pltpu.with_memory_space_constraint(value, pltpu.HBM)


def scatter_sum(y, axis, count, groups=None):
    y = y.reshape(count, y.shape[0] // count, 128)
    y = lax.all_to_all(y, axis, 0, 0, tiled=True, axis_index_groups=groups)
    return jnp.sum(y.astype(F32), 0).astype(BF16)


def spread(y, axis, count, groups=None):
    y = jnp.broadcast_to(y[None], (count,) + y.shape)
    return lax.all_to_all(y, axis, 0, 0, tiled=True, axis_index_groups=groups)


def local(volumes, w_first, w_down, w_coarse, cotangent):
    n, m = lax.axis_size("space"), lax.axis_size("dp")

    def swap(value, pairs):
        return lax.ppermute(value, "space", [p for i, j in pairs for p in ((i, j), (j, i))])

    chip = [(i, i + 1) for i in range(0, n, 2)]
    across = [(i, i + 1) for i in range(1, n - 1, 2)]
    beside = [[(i, i + 2) for i in range(n - 2) if i // 2 % 2 == k] for k in range(2)]
    first, last, inner, outer = call(
        edges_kernel,
        [((1280, 128), BF16)] * 4,
        [
            ((2, 64, 16, 128), BF16),
            ((64, 8, 64), BF16),
            ((2, 1024, 128), F32),
            ((512, 64), F32),
            pltpu.SemaphoreType.DMA((3,)),
        ],
        "hh",
    )(far(volumes.reshape(64, 2, 16, 128)), far(cotangent.reshape(64, 8, 64)))
    inner, outer = swap(inner, chip), swap(outer, across)
    part, fw, dw = call(
        prepare_kernel,
        [((1024, 256), F32), ((3072, 256), BF16), ((512, 128), BF16)],
        [
            ((512, 2048), BF16),
            ((1728, 64), BF16),
            ((512, 64), BF16),
            ((1728, 128), BF16),
            ((512, 128), BF16),
            pltpu.SemaphoreType.DMA((2,)),
        ],
        "vvhh",
    )(first, last, far(w_first.reshape(1728, 64)), far(w_down.reshape(512, 64)))
    act, slope, down, before, after = call(
        first_kernel,
        [((512, 512), BF16), ((1024, 256), F32), ((256, 128), BF16)] + [((1280, 128), BF16)] * 2,
        [((512, 1024), BF16)],
        "vvvvv",
    )(outer, inner, part, fw, dw)
    halo = [swap(down, pairs) for pairs in (across, beside[1], beside[0], chip)]
    cw, bw, ct, own, acc = call(
        beside_kernel,
        [
            ((3200, 256), BF16),
            ((64, 1920), BF16),
            ((512, 256), F32),
            ((512, 640), BF16),
            ((512, 256), F32),
        ],
        [((1728, 64), BF16), ((1728, 128), BF16), pltpu.SemaphoreType.DMA],
        "vvvvh",
    )(first, before, after, down, far(w_coarse.reshape(1728, 64)))
    out, keep, send = call(
        rest_kernel,
        [((64, 512), BF16), ((1024, 128), BF16), ((1024, 128), BF16)],
        [
            ((2048, 128), BF16),
            ((512, 1280), BF16),
            ((512, 1280), BF16),
            ((512, 1920), BF16),
            ((2048, 1024), BF16),
        ],
        16 * "v",
    )(*halo, first, last, before, after, act, slope, ct, own, acc, dw, cw, bw)
    half = (keep.astype(F32) + swap(send, chip).astype(F32)).astype(BF16)
    chips = [list(range(c, n, 2)) for c in range(2)]
    piece = scatter_sum(half, "dp", m)
    piece = jnp.sum(spread(piece, "space", n // 2, chips).astype(F32), 0).astype(BF16)
    mine = spread(piece, "dp", m).reshape(1024, 128)
    grad_first, grad_down, grad_coarse = call(
        unpack_kernel,
        [((3, 3, 3, 64, 64), F32), ((2, 2, 2, 64, 64), F32), ((3, 3, 3, 64, 64), F32)],
        [
            ((2048, 128), BF16),
            ((3, 3, 3, 64, 64), F32),
            ((2, 2, 2, 64, 64), F32),
            ((3, 3, 3, 64, 64), F32),
            pltpu.SemaphoreType.DMA((7,)),
        ],
        "vv",
        "hhh",
    )(mine, swap(mine, chip))
    return (out.reshape(1, 64, 1, 8, 64), grad_first, grad_down, grad_coarse)


def solution(mesh):
    return jax.shard_map(
        local,
        mesh=mesh,
        in_specs=(
            P("dp", None, "space", None, None),
            P(),
            P(),
            P(),
            P("dp", None, "space", None, None),
        ),
        out_specs=(P("dp", None, "space", None, None), P(), P(), P()),
        check_vma=False,
    )
```

```python
import jax
import jax.numpy as jnp
from jax import lax
from jax.experimental import pallas as pl
from jax.experimental.pallas import tpu as pltpu
from jax.sharding import PartitionSpec as P

F32, BF16 = jnp.float32, jnp.bfloat16
PARAMS = pltpu.CompilerParams(vmem_limit_bytes=32 * 1024 * 1024)
NN = (((1,), (0,)), ((), ()))
NT = (((1,), (1,)), ((), ()))


def dot(a, b, dims=NN):
    return lax.dot_general(a, b, dims, preferred_element_type=F32)


def core():
    return lax.axis_index("space") % 2


def low_lanes(shape):
    return lax.broadcasted_iota(jnp.int32, shape, 1) < 64


def pick_matrix():
    row = lax.broadcasted_iota(jnp.int32, (256, 128), 0)
    col = lax.broadcasted_iota(jnp.int32, (256, 128), 1)
    return (2 * (row % 64) - 1 + row // 64 == col).astype(F32).astype(BF16)


def twice():
    row = lax.broadcasted_iota(jnp.int32, (64, 128), 0)
    col = lax.broadcasted_iota(jnp.int32, (64, 128), 1)
    return (row == col % 64).astype(F32).astype(BF16)


def gather_taps(plane, out):
    picked = dot(pick_matrix(), plane, NT).astype(BF16)
    low = low_lanes((64, 128))
    zero = jnp.zeros((64, 128), BF16)
    for y in range(8):
        for tz in range(4):
            block = picked[tz * 64 : tz * 64 + 64]
            above = block[:, y * 128 - 128 : y * 128] if y > 0 else zero
            below = block[:, y * 128 + 128 : y * 128 + 256] if y < 7 else zero
            rows = slice(y * 64, y * 64 + 64)
            out[rows, tz * 128 : tz * 128 + 128] = block[:, y * 128 : y * 128 + 128]
            out[rows, 512 + tz * 128 : 640 + tz * 128] = jnp.where(low, below, above)


def gather_coarse(field, out):
    row = lax.broadcasted_iota(jnp.int32, (512, 128), 0) % 64
    low = low_lanes((512, 128))
    before = jnp.where(row == 0, 0.0, pltpu.roll(field, 1, 0))
    after = jnp.where(row == 63, 0.0, pltpu.roll(field, 511, 0))
    sides = jnp.where(low, before, after).astype(BF16)
    mid = field.astype(BF16)
    zero = jnp.zeros((64, 128), BF16)
    up = jnp.concatenate([zero, mid[:448]], 0)
    down = jnp.concatenate([mid[64:], zero], 0)
    out[0:64, 0:128] = zero
    out[64:512, 0:128] = sides[:448]
    out[:, 128:256] = sides
    out[0:448, 256:384] = sides[64:]
    out[448:512, 256:384] = zero
    out[:, 384:512] = jnp.where(low, up, down)
    out[:, 512:640] = mid


def turned(ref):
    field = ref.astype(F32)
    return field, pltpu.roll(field, 64, 1)


def doubled(ref):
    field, swapped = turned(ref)
    low = low_lanes((256, 128))
    return jnp.concatenate([jnp.where(low, field, swapped), jnp.where(low, swapped, field)], 0)


def edges_kernel(volumes, cot, first, last, inner, outer, raw, raw_cot, planes, rows, sems):
    copies = [pltpu.make_async_copy(volumes.at[:, x], raw.at[x], sems.at[x]) for x in range(2)]
    copies.append(pltpu.make_async_copy(cot, raw_cot, sems.at[2]))
    for copy in copies:
        copy.start()
    for x, out in enumerate((first, last)):
        copies[x].wait()
        planes[x] = raw[x].astype(F32).reshape(1024, 128)
        for y in range(16):
            out[y * 64 : y * 64 + 64] = planes[x, pl.ds(y, 64, stride=16), :].astype(BF16)
    copies[2].wait()
    rows[...] = raw_cot[...].astype(F32).reshape(512, 64)
    for j in range(4):
        both = jnp.concatenate(
            [rows[pl.ds(j, 64, stride=8), :], rows[pl.ds(j + 4, 64, stride=8), :]], 0
        )
        block = both.T.astype(BF16)
        for out in (first, last):
            out[1024 + j * 64 : 1088 + j * 64] = block
    even = core() == 0
    inner[...] = jnp.where(even, last[...], first[...])
    outer[...] = jnp.where(even, first[...], last[...])


def prepare_kernel(
    first, last, far_first, far_down, part, fw, dw, taps, w_first, w_down, sems
):
    weights = ((far_first, w_first), (far_down, w_down))
    copies = [pltpu.make_async_copy(far, to, sems.at[i]) for i, (far, to) in enumerate(weights)]
    for copy in copies:
        copy.start()
    low = low_lanes((64, 128))
    zero = jnp.zeros((64, 128), BF16)
    pair = twice()

    def both(ref, k):
        return dot(ref[k * 64 : k * 64 + 64], pair).astype(BF16)

    for x, ref in enumerate((first, last)):
        gather_taps(ref[0:1024], taps.at[:, x * 1024 : x * 1024 + 1024])
    for copy in copies:
        copy.wait()
    for dx in range(3):
        for iz in range(-1, 4):
            if 0 <= iz < 3:
                w = [both(w_first, dx * 9 + iy * 3 + iz) for iy in range(3)]
                blocks = (
                    (jnp.where(low, w[1], w[0]), jnp.where(low, w[2], w[1])),
                    (jnp.where(low, zero, w[2]), jnp.where(low, w[0], zero)),
                )
            else:
                blocks = ((zero, zero),) * 2
            for qz in range(2):
                tz = iz + qz
                for side in range(2 if 0 <= tz < 4 else 0):
                    at = dx * 1024 + side * 512 + tz * 128
                    for half in range(2):
                        rows = slice(at + half * 64, at + half * 64 + 64)
                        fw[rows, qz * 128 : qz * 128 + 128] = blocks[side][half]
    for x in range(2):
        for qz in range(2):
            for qy in range(2):
                k = x * 4 + qy * 2 + qz
                at = (x * 4 + qz * 2 + qy) * 64
                dw[at : at + 64] = both(w_down, k)
    for x in range(2):
        part[x * 512 : x * 512 + 512] = dot(taps[...], fw[1024 - x * 1024 : 3072 - x * 1024])


def first_kernel(outer, inner, part, fw, dw, act, slope, send, before, after, taps):
    low = low_lanes((256, 128))
    even = core() == 0
    before[...] = jnp.where(even, outer[...], inner[...])
    after[...] = jnp.where(even, inner[...], outer[...])
    for x, side in enumerate((before, after)):
        gather_taps(side[0:1024], taps)
        value = part[x * 512 : x * 512 + 512] + dot(taps[...], fw[x * 2048 : x * 2048 + 1024])
        s = jax.nn.sigmoid(value)
        slope[x * 512 : x * 512 + 512] = s * (1.0 + value * (1.0 - s))
        act[:, x * 256 : x * 256 + 256] = (value * s).astype(BF16)
    down = dot(act[...], dw[...])
    send[...] = jnp.where(low, down[:256], down[256:]).astype(BF16)


def beside_kernel(
    first, before, after, down, far_coarse, cw, bw, ct, own, acc, w_coarse, sem
):
    copy = pltpu.make_async_copy(far_coarse, w_coarse, sem)
    copy.start()
    low = low_lanes((256, 128))
    f0, t0 = turned(before[1024:1280])
    f1, t1 = turned(first[1024:1280])
    f2, t2 = turned(after[1024:1280])
    ct[0:256, 0:128] = jnp.where(low, f0, t1)
    ct[256:512, 0:128] = jnp.where(low, t0, f1)
    ct[0:256, 128:256] = f2
    ct[256:512, 128:256] = t2
    gather_coarse(doubled(down[...]), own)
    low = low_lanes((64, 128))
    zero = jnp.zeros((64, 128), BF16)
    pair = twice()

    def both(ref, k):
        return dot(ref[k * 64 : k * 64 + 64], pair).astype(BF16)

    copy.wait()
    order = [(0, 0), (0, 2), (1, 0), (1, 2), (2, 0), (2, 2), (0, 1), (2, 1), (1, 1), None]
    for j, tap in enumerate(order):
        if tap is None:
            w = [zero] * 3
        else:
            w = [both(w_coarse, dx * 9 + tap[0] * 3 + tap[1]) for dx in range(3)]
        w = [zero] * 2 + w + [zero] * 2
        for p in range(5):
            at = p * 640 + j * 64
            cw[at : at + 64, 0:128] = jnp.where(low, w[p + 2], w[p + 1])
            cw[at : at + 64, 128:256] = jnp.where(low, w[p], zero)
    for dx in range(3):
        back = [
            zero if tap is None else both(w_coarse, (2 - dx) * 9 + (2 - tap[0]) * 3 + 2 - tap[1])
            for tap in order
        ]
        for j in range(5):
            at = dx * 640 + j * 128
            bw[:, at : at + 128] = jnp.where(low, back[2 * j], back[2 * j + 1])
    acc[...] = dot(own[...], cw[1280:1920])


def rest_kernel(
    inner, chips0, chips1, outer, first, last, before, after, act, slope, ct, own, acc, dw, cw, bw, out, keep, send,
    grads, below, above, near, taps,
):
    low = low_lanes((64, 128))
    for p, ref in enumerate((before, first, last, after)):
        gather_taps(ref[0:1024], taps.at[p * 512 : p * 512 + 512])
    even, even_chip = core() == 0, lax.axis_index("space") // 2 % 2 == 0
    i, o, a, b = inner[...], outer[...], chips0[...], chips1[...]
    for p, plane in enumerate((jnp.where(even_chip, b, a), jnp.where(even, o, i))):
        gather_coarse(doubled(plane), below.at[:, p * 640 : p * 640 + 640])
    for p, plane in enumerate((jnp.where(even, i, o), jnp.where(even_chip, a, b))):
        gather_coarse(doubled(plane), above.at[:, p * 640 : p * 640 + 640])
    pre = acc[...] + dot(below[...], cw[0:1280]) + dot(above[...], cw[1920:3200])
    s = jax.nn.sigmoid(pre)
    out[...] = (pre[:, 0:128] * s[:, 0:128]).T[64:128].astype(BF16)
    grad = (ct[...] * (s * (1.0 + pre * (1.0 - s)))).astype(BF16).astype(F32)
    two, one = grad[:, 0:128], grad[:, 128:256]
    two_t, one_t = pltpu.roll(two, 64, 1), pltpu.roll(one, 64, 1)
    low2 = low_lanes((512, 128))
    gather_coarse(jnp.where(low2, two, two_t), near.at[:, 0:640])
    gather_coarse(jnp.where(low2, two_t, two), near.at[:, 640:1280])
    gather_coarse(jnp.where(low2, one, one_t), near.at[:, 1280:1920])
    dg_wide = dot(near[...], bw[...], NT)
    dg = dg_wide.astype(BF16)
    up = dot(dg, dw[:, 0:64], NT)
    fg_t = jnp.concatenate(
        [
            (up[:, x * 256 : x * 256 + 256] * slope[x * 512 : x * 512 + 512]).T.astype(BF16)
            for x in range(2)
        ],
        1,
    )
    mid_t = two.T[64:128].astype(BF16)
    center = []
    for dx, planes in enumerate((below[:, 640:1280], own[...], above[:, 0:640])):
        g = dot(mid_t, planes)
        for j in range(4):
            at = (14 + dx * 4 + j) * 64
            grads[at : at + 64] = g[:, j * 128 : j * 128 + 128].astype(BF16)
        center.append(g[:, 512:640])
    grads[26 * 64 : 27 * 64] = jnp.where(low, center[0], center[1]).astype(BF16)
    grads[27 * 64 : 28 * 64] = center[2].astype(BF16)
    gd = dot(dg_wide.T.astype(BF16), act[...])
    for j in range(4):
        at = (28 + j) * 64
        grads[at : at + 64] = gd[:, j * 128 : j * 128 + 128].astype(BF16)
    zero_y = []
    for dx in range(3):
        g = dot(fg_t, taps[dx * 512 : dx * 512 + 1024])
        for iz in range(3):

            def summed(side, qy):
                at = side * 512 + iz * 128
                return (
                    g[qy * 64 : qy * 64 + 64, at : at + 128]
                    + g[128 + qy * 64 : 192 + qy * 64, at + 128 : at + 256]
                )

            z0, z1, u0, u1 = summed(0, 0), summed(0, 1), summed(1, 0), summed(1, 1)
            j = dx * 3 + iz
            grads[j * 64 : j * 64 + 64] = (
                z0 + pltpu.roll(jnp.where(low, u1, z1), 64, 1)
            ).astype(BF16)
            zero_y.append((z1, u0))
    zero_y.append((jnp.zeros((64, 128), F32),) * 2)
    for m in range(5):
        (z1a, u0a), (z1b, u0b) = zero_y[2 * m], zero_y[2 * m + 1]
        at = (9 + m) * 64
        grads[at : at + 64] = (
            jnp.where(low, z1a, u0b) + pltpu.roll(jnp.where(low, z1b, u0a), 64, 1)
        ).astype(BF16)
    here = pl.multiple_of(core() * 1024, 1024)
    keep[...] = grads[pl.ds(here, 1024), :]
    send[...] = grads[pl.ds(pl.multiple_of(1024 - here, 1024), 1024), :]


def unpack_kernel(mine, other, far_first, far_down, far_coarse, packed, first, down, coarse, sems):
    here = pl.multiple_of(core() * 1024, 1024)
    packed[pl.ds(here, 1024), :] = mine[...]
    packed[pl.ds(pl.multiple_of(1024 - here, 1024), 1024), :] = other[...]
    copies = []

    def send(value, far):
        copies.append(pltpu.make_async_copy(value, far, sems.at[len(copies)]))
        copies[-1].start()

    def block(b):
        return packed[b * 64 : b * 64 + 64].astype(F32).T

    pairs = [((0, 0), (0, 2)), ((1, 0), (1, 2)), ((2, 0), (2, 2)), ((0, 1), (2, 1))]
    t, u = block(26), block(27)
    centers = (t[0:64], t[64:128], u[0:64])
    for dx in range(3):
        coarse[dx, 1, 1] = centers[dx]
        for j in range(4):
            t = block(14 + dx * 4 + j)
            for h in range(2):
                dy, dz = pairs[j][h]
                coarse[dx, dy, dz] = t[h * 64 : h * 64 + 64]
        send(coarse.at[dx], far_coarse.at[dx])
    for m in range(5):
        t = block(9 + m)
        for h in range(2):
            j = 2 * m + h
            if j < 9:
                first[j // 3, 0, j % 3] = t[h * 64 : h * 64 + 64]
    for dx in range(3):
        for iz in range(3):
            t = block(dx * 3 + iz)
            first[dx, 1, iz] = t[0:64]
            first[dx, 2, iz] = t[64:128]
        send(first.at[dx], far_first.at[dx])
    for j in range(4):
        t = block(28 + j)
        for qy in range(2):
            down[j // 2, qy, j % 2] = t[qy * 64 : qy * 64 + 64]
    send(down, far_down)
    for copy in copies:
        copy.wait()


def call(kernel, outs, scratch=(), places="", home=""):
    kinds = {"h": pltpu.HBM, "v": pltpu.VMEM}
    specs = {"in_specs": [pl.BlockSpec(memory_space=kinds[p]) for p in places]} if places else {}
    if home:
        specs["out_specs"] = [pl.BlockSpec(memory_space=kinds[p]) for p in home]
    return pl.pallas_call(
        kernel,
        out_shape=[jax.ShapeDtypeStruct(s, d) for s, d in outs],
        scratch_shapes=[pltpu.VMEM(*s) if isinstance(s, tuple) else s for s in scratch],
        compiler_params=PARAMS,
        **specs,
    )


def far(value):
    return pltpu.with_memory_space_constraint(value, pltpu.HBM)


def scatter_sum(y, axis, count, groups=None):
    y = y.reshape(count, y.shape[0] // count, 128)
    y = lax.all_to_all(y, axis, 0, 0, tiled=True, axis_index_groups=groups)
    return jnp.sum(y.astype(F32), 0).astype(BF16)


def spread(y, axis, count, groups=None):
    y = jnp.broadcast_to(y[None], (count,) + y.shape)
    return lax.all_to_all(y, axis, 0, 0, tiled=True, axis_index_groups=groups)


def local(volumes, w_first, w_down, w_coarse, cotangent):
    n, m = lax.axis_size("space"), lax.axis_size("dp")

    def swap(value, pairs):
        return lax.ppermute(value, "space", [p for i, j in pairs for p in ((i, j), (j, i))])

    chip = [(i, i + 1) for i in range(0, n, 2)]
    across = [(i, i + 1) for i in range(1, n - 1, 2)]
    beside = [[(i, i + 2) for i in range(n - 2) if i // 2 % 2 == k] for k in range(2)]
    first, last, inner, outer = call(
        edges_kernel,
        [((1280, 128), BF16)] * 4,
        [
            ((2, 64, 16, 128), BF16),
            ((64, 8, 64), BF16),
            ((2, 1024, 128), F32),
            ((512, 64), F32),
            pltpu.SemaphoreType.DMA((3,)),
        ],
        "hh",
    )(far(volumes.reshape(64, 2, 16, 128)), far(cotangent.reshape(64, 8, 64)))
    inner, outer = swap(inner, chip), swap(outer, across)
    part, fw, dw = call(
        prepare_kernel,
        [((1024, 256), F32), ((3072, 256), BF16), ((512, 128), BF16)],
        [((512, 2048), BF16), ((1728, 64), BF16), ((512, 64), BF16), pltpu.SemaphoreType.DMA((2,))],
        "vvhh",
    )(first, last, far(w_first.reshape(1728, 64)), far(w_down.reshape(512, 64)))
    act, slope, down, before, after = call(
        first_kernel,
        [((512, 512), BF16), ((1024, 256), F32), ((256, 128), BF16)] + [((1280, 128), BF16)] * 2,
        [((512, 1024), BF16)],
        "vvvvv",
    )(outer, inner, part, fw, dw)
    halo = [swap(down, pairs) for pairs in (chip, beside[0], beside[1], across)]
    cw, bw, ct, own, acc = call(
        beside_kernel,
        [
            ((3200, 256), BF16),
            ((64, 1920), BF16),
            ((512, 256), F32),
            ((512, 640), BF16),
            ((512, 256), F32),
        ],
        [((1728, 64), BF16), pltpu.SemaphoreType.DMA],
        "vvvvh",
    )(first, before, after, down, far(w_coarse.reshape(1728, 64)))
    out, keep, send = call(
        rest_kernel,
        [((64, 512), BF16), ((1024, 128), BF16), ((1024, 128), BF16)],
        [
            ((2048, 128), BF16),
            ((512, 1280), BF16),
            ((512, 1280), BF16),
            ((512, 1920), BF16),
            ((2048, 1024), BF16),
        ],
        16 * "v",
    )(*halo, first, last, before, after, act, slope, ct, own, acc, dw, cw, bw)
    half = (keep.astype(F32) + swap(send, chip).astype(F32)).astype(BF16)
    chips = [list(range(c, n, 2)) for c in range(2)]
    piece = scatter_sum(half, "dp", m)
    piece = jnp.sum(spread(piece, "space", n // 2, chips).astype(F32), 0).astype(BF16)
    mine = spread(piece, "dp", m).reshape(1024, 128)
    grad_first, grad_down, grad_coarse = call(
        unpack_kernel,
        [((3, 3, 3, 64, 64), F32), ((2, 2, 2, 64, 64), F32), ((3, 3, 3, 64, 64), F32)],
        [
            ((2048, 128), BF16),
            ((3, 3, 3, 64, 64), F32),
            ((2, 2, 2, 64, 64), F32),
            ((3, 3, 3, 64, 64), F32),
            pltpu.SemaphoreType.DMA((7,)),
        ],
        "vv",
        "hhh",
    )(mine, swap(mine, chip))
    return (out.reshape(1, 64, 1, 8, 64), grad_first, grad_down, grad_coarse)


def solution(mesh):
    return jax.shard_map(
        local,
        mesh=mesh,
        in_specs=(
            P("dp", None, "space", None, None),
            P(),
            P(),
            P(),
            P("dp", None, "space", None, None),
        ),
        out_specs=(P("dp", None, "space", None, None), P(), P(), P()),
        check_vma=False,
    )
```
